512 devices in a mesh: row: 32 (over x, y), col: 16 (over z, core).
Axes of the slice: x: 4, y: 8, z: 8, core: 2. Of those that a mesh axis runs over, the one named last changes fastest.
Arguments:
- right_hand: bfloat16 [16, 32, 512, 128], P('col', 'row'), may hold values from -6 to 6
- leaf_outer: bfloat16 [16, 32, 2, 512, 512], P('col', 'row'), may hold values from -0.21875 to 0.21875
- leaf_inner: bfloat16 [16, 32, 4, 256, 256], P('col', 'row')
- leaf_order: int32 [16, 32, 512], P('col', 'row'), may hold values from 0 to 511, each once within a row
- node_outer: bfloat16 [16, 32, 2, 512, 512], P('col', 'row'), may hold values from -0.21875 to 0.21875
- node_inner: bfloat16 [16, 32, 4, 256, 256], P('col', 'row')
- node_order: int32 [16, 32, 512], P('col', 'row'), may hold values from 0 to 511, each once within a row
Outputs:
- solution: bfloat16 [16, 32, 512, 128], P('col', 'row')
The draws below stay inside these ranges and needn't reach their ends.
Inputs may be any that keep to these rules, and one draw needn't show every extreme that they name: `leaf_order`: each row is a permutation of 0 to 511. `node_order`: each row is a permutation of 0 to 511.
All inputs are finite; a program needn't handle non-finite values.
Results may differ from the reference program's by a relative error of at most 0.04.
Values may be sent and summed in bfloat16 or wider, within the bound.
A program may use at most 64 MiB of HBM per device.

```python
import jax
import jax.numpy as jnp
import numpy as np
from jax import lax

LEAF = 512
R = 256
NRHS = 128
N_ROW = 32
N_COL = 16


def shape_blocks(noise):
    noise = noise * R ** (-0.5)
    row_ids = lax.broadcasted_iota(jnp.int32, (R, R), 0)
    col_ids = lax.broadcasted_iota(jnp.int32, (R, R), 1)
    identity = (row_ids == col_ids).astype(jnp.float32)
    lower_part = jnp.where(col_ids < row_ids, noise[:, :, 0], 0.0)
    upper_part = jnp.where(col_ids > row_ids, noise[:, :, 3], 0.0)
    coupling_up = 0.5 * noise[:, :, 1]
    coupling_down = 0.9 * noise[:, :, 2]
    return jnp.stack([identity + lower_part, coupling_up, coupling_down, identity + upper_part], axis=2)


def draw_leaf_inner(key, part):
    key = jax.random.fold_in(key, 11)
    noise = jax.random.normal(key, (N_COL, N_ROW, 4, R, R), jnp.float32)
    return shape_blocks(noise).astype(jnp.bfloat16)


def draw_node_inner(key, part):
    key = jax.random.fold_in(key, 23)
    noise = jax.random.normal(key, (N_COL, N_ROW, 4, R, R), jnp.float32)
    return shape_blocks(noise).astype(jnp.bfloat16)


def steps_of(own_key, shape, cuts, smallest, high):
    def one(dim, shards_of):
        steps = jax.random.uniform(jax.random.fold_in(jax.random.fold_in(own_key, 6), dim), (shards_of,), jnp.float32, smallest / len(cuts), high / len(cuts))
        return jnp.repeat(jnp.exp(steps), shape[dim] // shards_of).reshape((-1,) + (1,) * (len(shape) - dim - 1))

    loudness = one(*cuts[0])
    for cut in cuts[1:]:
        loudness = loudness * one(*cut)
    return loudness


def bell_draw(rng, dims, deviation, limit, shards=(), kind=jnp.bfloat16):
    factor_of = steps_of(rng, dims, shards, -0.22, 0.18) if shards else 1.0
    entries = jax.random.normal(rng, dims, jnp.float32) * deviation * factor_of
    return jnp.minimum(jnp.maximum(entries, -limit), limit).astype(kind)


def setup_inputs(seed: int = 0) -> dict:
    key_list = jax.random.split(jax.random.key(seed), 8)
    right_hand = bell_draw(key_list[0], (N_COL, N_ROW, LEAF, NRHS), 1.0, 6.0, ((0, 16), (1, 32)))
    leaf_outer = bell_draw(key_list[1], (N_COL, N_ROW, 2, LEAF, LEAF), (4 * LEAF // 3) ** -0.5, 0.21875, ((0, 16), (1, 32)))
    leaf_inner = draw_leaf_inner(jax.random.fold_in(key_list[7], 71), 0)
    leaf_order = jax.vmap(lambda own: jax.random.permutation(own, LEAF))(jax.random.split(key_list[3], N_COL * N_ROW)).reshape((N_COL, N_ROW, LEAF)).astype(jnp.int32)
    node_outer = bell_draw(key_list[4], (N_COL, N_ROW, 2, LEAF, LEAF), (4 * LEAF // 3) ** -0.5, 0.21875, ((0, 16), (1, 32)))
    node_inner = draw_node_inner(jax.random.fold_in(key_list[7], 71), 0)
    node_order = jax.vmap(lambda own: jax.random.permutation(own, LEAF))(jax.random.split(key_list[6], N_COL * N_ROW)).reshape((N_COL, N_ROW, LEAF)).astype(jnp.int32)
    return {"right_hand": right_hand, "leaf_outer": leaf_outer, "leaf_inner": leaf_inner, "leaf_order": leaf_order, "node_outer": node_outer, "node_inner": node_inner, "node_order": node_order}


HIGHEST_MODE = lax.Precision.HIGHEST


def product(left_side, right_side):
    return jnp.dot(left_side.astype(jnp.float32), right_side.astype(jnp.float32), precision=HIGHEST_MODE)


def forward(packed):
    outer_pair, inner_four, ordering, vector = packed
    rotated = jnp.take(product(outer_pair[0], vector), ordering, axis=0)
    eliminated = rotated[:R].astype(jnp.bfloat16)
    reduced = product(inner_four[0], eliminated).astype(jnp.bfloat16)
    skeleton = (rotated[R:] - product(inner_four[1], reduced)).astype(jnp.bfloat16)
    return skeleton, reduced


def backward(packed):
    outer_pair, inner_four, ordering, reduced, incoming = packed
    target = (reduced.astype(jnp.float32) - product(inner_four[2], incoming)).astype(jnp.bfloat16)
    solved = product(inner_four[3], target).astype(jnp.bfloat16)
    stacked = jnp.concatenate([solved, incoming], axis=0)
    placed = jnp.zeros_like(stacked).at[ordering].set(stacked)
    return product(outer_pair[1], placed).astype(jnp.bfloat16)


def spans(extent):
    result = []
    level_span = 2
    while level_span <= extent:
        result.append(level_span)
        level_span = level_span * 2
    return result


def layout(extent, level_span):
    owners = np.arange(level_span // 2 - 1, extent, level_span)
    if level_span == 2:
        return owners, owners, owners + 1
    return owners, owners - level_span // 4, owners + level_span // 4


def climb(skeleton, outer_pair, inner_four, ordering, extent):
    stored = jnp.zeros_like(skeleton)
    for level_span in spans(extent):
        owners, left_slots, right_slots = layout(extent, level_span)
        vectors = jnp.concatenate([skeleton[left_slots], skeleton[right_slots]], axis=1)
        new_skeleton, new_reduced = lax.map(forward, (outer_pair[owners], inner_four[owners], ordering[owners], vectors))
        skeleton = skeleton.at[owners].set(new_skeleton)
        stored = stored.at[owners].set(new_reduced)
    return skeleton, stored


def descend(incoming, stored, outer_pair, inner_four, ordering, extent):
    for level_span in reversed(spans(extent)):
        owners, left_slots, right_slots = layout(extent, level_span)
        values = lax.map(backward, (outer_pair[owners], inner_four[owners], ordering[owners], stored[owners], incoming[owners]))
        incoming = incoming.at[left_slots].set(values[:, :R])
        incoming = incoming.at[right_slots].set(values[:, R:])
    return incoming


def reference(right_hand, leaf_outer, leaf_inner, leaf_order, node_outer, node_inner, node_order):
    leaf_count = N_COL * N_ROW
    flat_outer = leaf_outer.reshape(leaf_count, 2, LEAF, LEAF)
    flat_inner = leaf_inner.reshape(leaf_count, 4, R, R)
    flat_order = leaf_order.reshape(leaf_count, LEAF)
    flat_right = right_hand.reshape(leaf_count, LEAF, NRHS)
    leaf_skeleton, leaf_reduced = lax.map(forward, (flat_outer, flat_inner, flat_order, flat_right))
    leaf_skeleton = leaf_skeleton.reshape(N_COL, N_ROW, R, NRHS)
    column_roots = []
    column_stores = []
    for column in range(N_COL):
        skeleton, stored = climb(leaf_skeleton[column], node_outer[column], node_inner[column], node_order[column], N_ROW)
        column_roots.append(skeleton[N_ROW // 2 - 1])
        column_stores.append(stored)
    upper_skeleton = jnp.stack(column_roots, axis=0)
    upper_outer = node_outer[:, N_ROW - 1]
    upper_inner = node_inner[:, N_ROW - 1]
    upper_order = node_order[:, N_ROW - 1]
    upper_skeleton, upper_stored = climb(upper_skeleton, upper_outer, upper_inner, upper_order, N_COL)
    top_value = product(node_inner[N_COL - 1, N_ROW - 1, 0], upper_skeleton[N_COL // 2 - 1]).astype(jnp.bfloat16)
    upper_incoming = jnp.zeros((N_COL, R, NRHS), jnp.bfloat16).at[N_COL // 2 - 1].set(top_value)
    upper_incoming = descend(upper_incoming, upper_stored, upper_outer, upper_inner, upper_order, N_COL)
    leaf_incoming = []
    for column in range(N_COL):
        incoming = jnp.zeros((N_ROW, R, NRHS), jnp.bfloat16).at[N_ROW // 2 - 1].set(upper_incoming[column])
        incoming = descend(incoming, column_stores[column], node_outer[column], node_inner[column], node_order[column], N_ROW)
        leaf_incoming.append(incoming)
    flat_incoming = jnp.stack(leaf_incoming, axis=0).reshape(leaf_count, R, NRHS)
    solution = lax.map(backward, (flat_outer, flat_inner, flat_order, leaf_reduced, flat_incoming))
    return solution.reshape(N_COL, N_ROW, LEAF, NRHS)
```

```python
import functools

import jax
import jax.numpy as jnp
from jax import lax
from jax.experimental import pallas as pl
from jax.experimental.pallas import tpu as pltpu
from jax.sharding import PartitionSpec as P

MESH = pl.DeviceIdType.MESH
BF16 = jnp.bfloat16
F32 = jnp.float32
RANK = 256
ROWS = 512
RHS = 128


def mm(a, b):
    return jnp.dot(a, b, preferred_element_type=F32)


def one_hot(order_ref):
    rows = lax.broadcasted_iota(jnp.int32, (ROWS, ROWS), 0)
    return jnp.where(rows == order_ref[...], 1.0, 0.0).astype(BF16)


def gather_rows(hot, block):
    return lax.dot_general(hot, block, (((0,), (0,)), ((), ())), preferred_element_type=F32)


def level_of(place):
    p = place + 1
    level = jnp.int32(2)
    for k in (2, 4, 8, 16):
        level = jnp.where(lax.rem(p, k) == 0, 2 * k, level)
    return level


def kernel(
    rows,
    cols,
    rhs_h,
    lo_h,
    li_h,
    lord_h,
    no_h,
    ni_h,
    nord_h,
    out,
    rhs,
    lo,
    li,
    lord,
    no,
    ni,
    nord,
    skel_leaf,
    merged,
    skel_node,
    top,
    inc_node,
    inc_leaf,
    values,
    s_mat,
    h_node,
    g_node,
    h_leaf,
    g_leaf,
    p1,
    q1,
    load_sem,
    send_sem,
    recv_sem,
):
    r = lax.axis_index("row")
    c = lax.axis_index("col")
    last = r == rows - 1
    place = jnp.where(last, c, r)
    g = level_of(place)
    extent = jnp.where(last, cols, rows)
    has_node = jnp.logical_not(last & (c == cols - 1))
    is_root = last & (c == cols // 2 - 1)
    odd = lax.rem(r, 2) == 1
    pair = jnp.logical_not(last) & (g == 2)
    start = place + 1 - g // 2
    side = lax.rem(start // g, 2)
    up_place = start - side * g + g - 1
    col_root = jnp.logical_not(last) & (g == rows)
    up_row = jnp.where(col_root | last, rows - 1, up_place)
    up_col = jnp.where(last, up_place, jnp.where(col_root, c - lax.rem(c, 2), c))
    side = jnp.where(col_root, lax.rem(c, 2), side)
    reach = g // 4
    upper2 = last & (g == 2)
    left_row = jnp.where(upper2, rows // 2 - 1, jnp.where(last, r, r - reach))
    left_col = jnp.where(last, jnp.where(upper2, c, c - reach), c)
    right_row = jnp.where(upper2, rows // 2 - 1, jnp.where(last, r, r + reach))
    right_col = jnp.where(last, jnp.where(upper2, c + 1, c + reach), c)
    up_dev = (up_row, up_col)
    left_dev = (left_row, left_col)
    right_dev = (right_row, right_col)
    is_top_block = last & (c == cols - 1)
    top_dev = (r, jnp.int32(cols // 2 - 1))
    block_dev = (r, jnp.int32(cols - 1))

    loads = [
        (lord_h.at[0], lord),
        (lo_h.at[0, 0, 0], lo.at[0]),
        (rhs_h.at[0, 0], rhs),
        (li_h.at[0, 0, pl.ds(0, 2)], li.at[pl.ds(0, 2)]),
        (nord_h.at[0], nord),
        (no_h.at[0, 0, 0], no.at[0]),
        (ni_h.at[0, 0, pl.ds(0, 2)], ni.at[pl.ds(0, 2)]),
        (lo_h.at[0, 0, 1], lo.at[1]),
        (li_h.at[0, 0, pl.ds(2, 2)], li.at[pl.ds(2, 2)]),
        (no_h.at[0, 0, 1], no.at[1]),
        (ni_h.at[0, 0, pl.ds(2, 2)], ni.at[pl.ds(2, 2)]),
    ]
    copies = [
        pltpu.make_async_copy(src, dst, load_sem.at[i]) for i, (src, dst) in enumerate(loads)
    ]
    for copy in copies:
        copy.start()

    barrier = pltpu.get_barrier_semaphore()

    def greet(dev):
        pl.semaphore_signal(barrier, inc=1, device_id=dev, device_id_type=MESH)

    def greet_if(cond, dev):
        @pl.when(cond)
        def _():
            greet(dev)

    two_children = has_node & jnp.logical_not(pair)
    has_up = has_node & jnp.logical_not(is_root)
    greet_if(odd, (r - 1, c))
    greet_if(pair, (r + 1, c))
    greet_if(two_children, left_dev)
    greet_if(two_children, right_dev)
    greet_if(has_up, up_dev)
    greet_if(is_top_block, top_dev)
    greet_if(is_root, block_dev)

    def remote(src, dst, i, j, dev):
        return pltpu.make_async_remote_copy(
            src_ref=src,
            dst_ref=dst,
            send_sem=send_sem.at[i],
            recv_sem=recv_sem.at[j],
            device_id=dev,
            device_id_type=MESH,
        )

    lower = pl.ds(0, RANK)
    upper = pl.ds(RANK, RANK)
    halves = (lower, upper)

    copies[0].wait()
    hot_leaf = one_hot(lord)
    copies[1].wait()
    copies[2].wait()
    rotated = mm(lo[0], rhs[...])
    high = rotated.astype(BF16)
    low = (rotated - high.astype(F32)).astype(BF16)
    both = gather_rows(hot_leaf, jnp.concatenate([high, low], axis=1))
    rotated = both[:, :RHS] + both[:, RHS:]
    copies[3].wait()
    leaf_reduced = mm(li[0], rotated[:RANK].astype(BF16)).astype(BF16)
    skel_leaf[...] = (rotated[RANK:] - mm(li[1], leaf_reduced)).astype(BF16)

    waits = jnp.where(odd, 1, 0) + jnp.where(pair, 1, 0) + jnp.where(two_children, 2, 0)
    waits = waits + jnp.where(has_up, 1, 0) + jnp.where(is_top_block | is_root, 1, 0)
    pl.semaphore_wait(barrier, waits)

    leaf_up = remote(skel_leaf, merged.at[upper], 0, 1, (r - 1, c))

    @pl.when(odd)
    def _():
        leaf_up.start()

    @pl.when(jnp.logical_not(odd))
    def _():
        merged[lower] = skel_leaf[...]

    copies[6].wait()
    top_copy = remote(ni.at[0], top, 1, 4, top_dev)

    @pl.when(is_top_block)
    def _():
        top_copy.start()

    copies[4].wait()
    hot_node = one_hot(nord)
    copies[5].wait()
    gathered = gather_rows(hot_node, no[0])
    p1[...] = gathered[:RANK].astype(BF16)
    el = mm(ni[1], ni[0]).astype(BF16)
    s_mat[...] = (gathered[RANK:] - mm(el, p1[...])).astype(BF16)

    @pl.when(two_children)
    def _():
        remote(merged.at[lower], merged.at[lower], 2, 0, left_dev).wait_recv()

    @pl.when(has_node)
    def _():
        remote(merged.at[upper], merged.at[upper], 2, 1, right_dev).wait_recv()
        skel_node[...] = mm(s_mat[...], merged[...]).astype(BF16)

    up_left = remote(skel_node, merged.at[lower], 2, 0, up_dev)
    up_right = remote(skel_node, merged.at[upper], 2, 1, up_dev)

    @pl.when(has_up & (side == 0))
    def _():
        up_left.start()

    @pl.when(has_up & (side == 1))
    def _():
        up_right.start()

    copies[9].wait()
    copies[10].wait()
    placed = mm(no[1], hot_node).astype(BF16)
    q1[...] = placed[:, :RANK]
    uf = mm(ni[3], ni[2]).astype(BF16)
    h_node[...] = (placed[:, RANK:].astype(F32) - mm(q1[...], uf)).astype(BF16)

    @pl.when(has_node)
    def _():
        eliminated = mm(p1[...], merged[...]).astype(BF16)
        reduced = mm(ni[0], eliminated).astype(BF16)
        solved = mm(ni[3], reduced).astype(BF16)
        g_node[...] = mm(q1[...], solved)

    copies[7].wait()
    copies[8].wait()
    placed = mm(lo[1], hot_leaf).astype(BF16)
    first = placed[:, :RANK]
    uf = mm(li[3], li[2]).astype(BF16)
    h_leaf[...] = (placed[:, RANK:].astype(F32) - mm(first, uf)).astype(BF16)
    g_leaf[...] = mm(first, mm(li[3], leaf_reduced).astype(BF16))

    @pl.when(is_root)
    def _():
        remote(top, top, 1, 4, block_dev).wait_recv()
        inc_node[...] = mm(top[...], skel_node[...]).astype(BF16)

    @pl.when(has_up)
    def _():
        remote(inc_node, inc_node, 2, 2, up_dev).wait_recv()

    @pl.when(has_node)
    def _():
        values[...] = (g_node[...] + mm(h_node[...], inc_node[...])).astype(BF16)

    down_left = remote(values.at[lower], inc_node, 3, 2, left_dev)
    down_right = remote(values.at[upper], inc_node, 4, 2, right_dev)
    down_leaf = remote(values.at[upper], inc_leaf, 4, 3, (r + 1, c))

    @pl.when(two_children)
    def _():
        down_left.start()
        down_right.start()

    @pl.when(pair)
    def _():
        down_leaf.start()
        inc_leaf[...] = values[lower]

    @pl.when(odd)
    def _():
        remote(inc_leaf, inc_leaf, 0, 3, (r - 1, c)).wait_recv()

    out[0, 0] = (g_leaf[...] + mm(h_leaf[...], inc_leaf[...])).astype(BF16)

    @pl.when(odd)
    def _():
        leaf_up.wait_send()

    @pl.when(is_top_block)
    def _():
        top_copy.wait_send()

    @pl.when(has_up)
    def _():
        up_left.wait_send()

    @pl.when(two_children)
    def _():
        down_left.wait_send()
        down_right.wait_send()

    @pl.when(pair)
    def _():
        down_leaf.wait_send()


def solution(mesh):
    rows, cols = mesh.shape["row"], mesh.shape["col"]
    vm = pltpu.VMEM
    scratch = [
        vm((ROWS, RHS), BF16),
        vm((2, ROWS, ROWS), BF16),
        vm((4, RANK, RANK), BF16),
        vm((1, ROWS), jnp.int32),
        vm((2, ROWS, ROWS), BF16),
        vm((4, RANK, RANK), BF16),
        vm((1, ROWS), jnp.int32),
        vm((RANK, RHS), BF16),
        vm((ROWS, RHS), BF16),
        vm((RANK, RHS), BF16),
        vm((RANK, RANK), BF16),
        vm((RANK, RHS), BF16),
        vm((RANK, RHS), BF16),
        vm((ROWS, RHS), BF16),
        vm((RANK, ROWS), BF16),
        vm((ROWS, RANK), BF16),
        vm((ROWS, RHS), F32),
        vm((ROWS, RANK), BF16),
        vm((ROWS, RHS), F32),
        vm((RANK, ROWS), BF16),
        vm((ROWS, RANK), BF16),
        pltpu.SemaphoreType.DMA((11,)),
        pltpu.SemaphoreType.DMA((5,)),
        pltpu.SemaphoreType.DMA((5,)),
    ]
    call = pl.pallas_call(
        functools.partial(kernel, rows, cols),
        out_shape=jax.ShapeDtypeStruct((1, 1, ROWS, RHS), BF16),
        in_specs=[pl.BlockSpec(memory_space=pl.ANY)] * 7,
        out_specs=pl.BlockSpec(memory_space=pltpu.VMEM),
        scratch_shapes=scratch,
        compiler_params=pltpu.CompilerParams(
            collective_id=0, has_side_effects=True, vmem_limit_bytes=62 * 1024 * 1024
        ),
        name="tree",
    )
    in_specs = (
        P("col", "row", None, None),
        P("col", "row", None, None, None),
        P("col", "row", None, None, None),
        P("col", "row", None),
        P("col", "row", None, None, None),
        P("col", "row", None, None, None),
        P("col", "row", None),
    )
    out_specs = P("col", "row", None, None)
    return jax.shard_map(call, mesh=mesh, in_specs=in_specs, out_specs=out_specs, check_vma=False)
```

```python
import functools

import jax
import jax.numpy as jnp
from jax import lax
from jax.experimental import pallas as pl
from jax.experimental.pallas import tpu as pltpu
from jax.sharding import PartitionSpec as P

MESH = pl.DeviceIdType.MESH
BF16 = jnp.bfloat16
F32 = jnp.float32
RANK = 256
ROWS = 512
RHS = 128


def mm(a, b):
    return jnp.dot(a, b, preferred_element_type=F32)


def one_hot(order_ref):
    rows = lax.broadcasted_iota(jnp.int32, (ROWS, ROWS), 0)
    return jnp.where(rows == order_ref[...], 1.0, 0.0).astype(BF16)


def gather_rows(hot, block):
    return lax.dot_general(hot, block, (((0,), (0,)), ((), ())), preferred_element_type=F32)


class Message:
    def __init__(self, net, out_cond, dst, in_cond, src, slot):
        self.net, self.out_cond, self.dst, self.in_cond, self.src = net, out_cond, dst, in_cond, src
        self.slot, self.lane = slot, len(net.messages)
        net.messages.append(self)

    def start(self, src_ref, dst_ref):
        self.copy = pltpu.make_async_remote_copy(
            src_ref=src_ref,
            dst_ref=dst_ref,
            send_sem=self.net.send_sem.at[self.lane],
            recv_sem=self.net.recv_sem.at[self.slot],
            device_id=self.dst,
            device_id_type=MESH,
        )
        pl.when(self.out_cond)(self.copy.start)

    def finish(self):
        pl.when(self.out_cond)(self.copy.wait_send)


class Net:
    def __init__(self, send_sem, recv_sem):
        self.messages, self.send_sem, self.recv_sem = [], send_sem, recv_sem
        c = lax.axis_index("col")
        self.partner = (lax.axis_index("row"), c + 1 - 2 * lax.rem(c, 2))

    def add(self, out_cond, dst, in_cond, src, slot):
        return Message(self, out_cond, dst, in_cond, src, slot)

    def greet(self):
        barrier = pltpu.get_barrier_semaphore()
        for m in self.messages:

            @pl.when(m.in_cond)
            def _(m=m):
                pl.semaphore_signal(barrier, inc=1, device_id=m.src, device_id_type=MESH)

    def meet(self):
        count = sum(jnp.where(m.out_cond, 1, 0) for m in self.messages)
        pl.semaphore_wait(pltpu.get_barrier_semaphore(), count)

    def arrived(self, cond, ref, slot):
        copy = pltpu.make_async_remote_copy(
            src_ref=ref,
            dst_ref=ref,
            send_sem=self.send_sem.at[0],
            recv_sem=self.recv_sem.at[slot],
            device_id=self.partner,
            device_id_type=MESH,
        )
        pl.when(cond)(copy.wait_recv)

    def finish(self):
        for m in self.messages:
            m.finish()


MESSAGES = 60
(
    B_LEFT,
    B_RIGHT,
    INC,
    INC_LEAF,
    TOP,
    HB_LEFT,
    HB_RIGHT,
    S_HUB,
    M_HUB,
    S_HALF,
    K_HUB,
    PART_0,
    PART_1,
    PART_2,
    LOC_HUB,
    INC_ROOT,
    INC_HUB,
    K_NODE,
    K_LEAF,
    M_TOP,
    S_OTHER,
    M_FOUR,
    PEER_1,
    PEER_2,
    PEER_3,
) = range(25)
SLOTS = 25


def kernel(
    rhs_h, lo_h, li_h, lord_h, no_h, ni_h, nord_h, out,
    rhs, lo, li, lord, no, ni, nord,
    leaf_reduced, skel_leaf, merged, skel_node, top, inc_node, inc_leaf, values,
    s_mat, h_node, g_node, h_leaf, g_leaf, p1, q1,
    hb, s_hub, m_hub, m_out, s_half, k_hub, parts, part_own, skel_hub, skel_eight, cm, loc_hub,
    inc_root, inc_hub, k_node, k_leaf, kv, big_g, m_top, m_in, s_other, m_four, m_rows, peers, skel_root,
    load_sem, send_sem, recv_sem,
):
    r = lax.axis_index("row")
    c = lax.axis_index("col")
    x = r // 8
    y = lax.rem(r, 8)
    even = lax.rem(y, 2) == 0
    odd = jnp.logical_not(even)
    n2 = even
    n4 = (y == 1) | (y == 5)
    n8 = y == 3
    hub = y == 7
    n16 = hub & ((x == 0) | (x == 2))
    n32 = hub & (x == 1)
    last = hub & (x == 3)
    col_even = last & (lax.rem(c, 2) == 0)
    col_odd = last & (lax.rem(c, 2) == 1)
    u2 = col_even
    u4 = last & (lax.rem(c, 4) == 1)
    u8 = last & (lax.rem(c, 8) == 3)
    u16 = last & (c == 7)
    block = last & (c == 15)
    node = jnp.logical_not(u8 | u16 | block)
    lead = hub & jnp.logical_not(n16)

    loads = [
        (lord_h.at[0], lord),
        (lo_h.at[0, 0, 0], lo.at[0]),
        (rhs_h.at[0, 0], rhs),
        (li_h.at[0, 0, pl.ds(0, 2)], li.at[pl.ds(0, 2)]),
        (nord_h.at[0], nord),
        (no_h.at[0, 0, 0], no.at[0]),
        (ni_h.at[0, 0, pl.ds(0, 2)], ni.at[pl.ds(0, 2)]),
        (no_h.at[0, 0, 1], no.at[1]),
        (ni_h.at[0, 0, pl.ds(2, 2)], ni.at[pl.ds(2, 2)]),
        (lo_h.at[0, 0, 1], lo.at[1]),
        (li_h.at[0, 0, pl.ds(2, 2)], li.at[pl.ds(2, 2)]),
    ]
    copies = [
        pltpu.make_async_copy(src, dst, load_sem.at[i]) for i, (src, dst) in enumerate(loads)
    ]
    for copy in copies:
        copy.start()

    net = Net(send_sem, recv_sem)
    add = net.add
    leaf_up = add(odd, (r - 1, c), even, (r + 1, c), B_RIGHT)
    n2_left = add((y == 0) | (y == 4), (r + 1, c), n4, (r - 1, c), B_LEFT)
    n2_right = add((y == 2) | (y == 6), (r - 1, c), n4, (r + 1, c), B_RIGHT)
    n4_hub_left = add(y == 1, (r + 6, c), hub, (r - 6, c), HB_LEFT)
    n4_hub_right = add(y == 5, (r + 2, c), hub, (r - 2, c), HB_RIGHT)
    n4_left = add(y == 1, (r + 2, c), n8, (r - 2, c), B_LEFT)
    n4_right = add(y == 5, (r - 2, c), n8, (r + 2, c), B_RIGHT)
    s_to_hub = add(n8, (r + 4, c), hub, (r - 4, c), S_HUB)
    s_left = add(n32, (r - 8, c), hub & (x == 0), (r + 8, c), S_HALF)
    s_right = add(n32, (r + 8, c), hub & (x == 2), (r - 8, c), S_HALF)
    m_to_hub = add(n16, (r + 8, c), lead, (r - 8, c), M_HUB)
    part_to_root = [
        add(hub & (x == i), (31, c), last, (8 * i + 7, c), PART_0 + i) for i in range(3)
    ]
    n8_up = add(lead, (r - 8, c), n16, (r + 8, c), B_RIGHT)
    n16_left = add(hub & (x == 0), (r + 8, c), n32, (r - 8, c), B_LEFT)
    n16_right = add(hub & (x == 2), (r - 8, c), n32, (r + 8, c), B_RIGHT)
    col_up = add(col_odd, (r, c - 1), col_even, (r, c + 1), B_RIGHT)
    u2_left = add(last & (lax.rem(c, 4) == 0), (r, c + 1), u4, (r, c - 1), B_LEFT)
    u2_right = add(last & (lax.rem(c, 4) == 2), (r, c - 1), u4, (r, c + 1), B_RIGHT)
    peer = [
        add(u4, (r, lax.rem(c + 4 * k, 16)), u4, (r, lax.rem(c + 16 - 4 * k, 16)), PEER_1 + k - 1)
        for k in (2, 1, 3)
    ]
    top_send = add(block, (r, c - 8), u16, (r, c + 8), TOP)
    m_top_left = add(u16, (r, c - 4), last & (c == 3), (r, c + 4), M_TOP)
    m_top_right = add(u16, (r, c + 4), last & (c == 11), (r, c - 4), M_TOP)
    s_exchange = add(u8, (r, lax.rem(c + 8, 16)), u8, (r, lax.rem(c + 8, 16)), S_OTHER)
    m_four_left = add(u8, (r, c - 2), last & (lax.rem(c, 8) == 1), (r, c + 2), M_FOUR)
    m_four_right = add(u8, (r, c + 2), last & (lax.rem(c, 8) == 5), (r, c - 2), M_FOUR)
    n32_down_left = add(n32, (r - 8, c), hub & (x == 0), (r + 8, c), INC)
    n32_down_right = add(n32, (r + 8, c), hub & (x == 2), (r - 8, c), INC)
    n16_down = add(n16, (r + 8, c), lead, (r - 8, c), LOC_HUB)
    n8_down_left = add(n8, (r - 2, c), y == 1, (r + 2, c), INC)
    n8_down_right = add(n8, (r + 2, c), y == 5, (r - 2, c), INC)
    n4_down_left = add(n4, (r - 1, c), (y == 0) | (y == 4), (r + 1, c), INC)
    n4_down_right = add(n4, (r + 1, c), (y == 2) | (y == 6), (r - 1, c), INC)
    n2_down = add(n2, (r + 1, c), odd, (r - 1, c), INC_LEAF)
    u4_down_left = add(u4, (r, c - 1), last & (lax.rem(c, 4) == 0), (r, c + 1), INC)
    u4_down_right = add(u4, (r, c + 1), last & (lax.rem(c, 4) == 2), (r, c - 1), INC)
    u2_down = add(u2, (r, c + 1), col_odd, (r, c - 1), INC_ROOT)
    n32_k_left = add(n32, (r - 8, c), hub & (x == 0), (r + 8, c), K_NODE)
    n32_k_right = add(n32, (r + 8, c), hub & (x == 2), (r - 8, c), K_NODE)
    n16_k = add(n16, (r + 8, c), lead, (r - 8, c), K_HUB)
    n8_k_left = add(n8, (r - 2, c), y == 1, (r + 2, c), K_NODE)
    n8_k_right = add(n8, (r + 2, c), y == 5, (r - 2, c), K_NODE)
    n4_k_left = add(n4, (r - 1, c), (y == 0) | (y == 4), (r + 1, c), K_NODE)
    n4_k_right = add(n4, (r + 1, c), (y == 2) | (y == 6), (r - 1, c), K_NODE)
    n2_k = add(n2, (r + 1, c), odd, (r - 1, c), K_LEAF)
    root_down = [add(last, (8 * i + 7, c), hub & (x == i), (31, c), INC_ROOT) for i in (1, 0, 2)]
    hub_down = [
        add(hub, (8 * x + i, c), y == i, (8 * x + 7, c), INC_HUB) for i in (3, 2, 4, 1, 5, 0, 6)
    ]
    net.greet()

    lower = pl.ds(0, RANK)
    upper = pl.ds(RANK, RANK)

    copies[0].wait()
    hot_leaf = one_hot(lord)
    copies[1].wait()
    copies[2].wait()
    rotated = mm(lo[0], rhs[...])
    high = rotated.astype(BF16)
    low = (rotated - high.astype(F32)).astype(BF16)
    both = gather_rows(hot_leaf, jnp.concatenate([high, low], axis=1))
    rotated = both[:, :RHS] + both[:, RHS:]
    copies[3].wait()
    leaf_reduced[...] = mm(li[0], rotated[:RANK].astype(BF16)).astype(BF16)
    skel_leaf[...] = (rotated[RANK:] - mm(li[1], leaf_reduced[...])).astype(BF16)

    net.meet()
    leaf_up.start(skel_leaf, merged.at[upper])

    @pl.when(even)
    def _():
        merged[lower] = skel_leaf[...]

    copies[6].wait()
    top_send.start(ni.at[0], top)

    copies[4].wait()
    hot_node = one_hot(nord)
    copies[5].wait()
    gathered = gather_rows(hot_node, no[0])
    p1[...] = gathered[:RANK].astype(BF16)
    el = mm(ni[1], ni[0]).astype(BF16)
    s_mat[...] = (gathered[RANK:] - mm(el, p1[...])).astype(BF16)
    s_to_hub.start(s_mat, s_hub)
    s_left.start(s_mat.at[:, lower], s_half)
    s_right.start(s_mat.at[:, upper], s_half)
    s_exchange.start(s_mat, s_other)

    def leaf_down():
        placed = mm(lo[1], one_hot(lord)).astype(BF16)
        first = placed[:, :RANK]
        uf = mm(li[3], li[2]).astype(BF16)
        h = (placed[:, RANK:].astype(F32) - mm(first, uf)).astype(BF16)
        reduced = leaf_reduced[...]
        net.arrived(odd, inc_leaf, INC_LEAF)
        g = mm(first, mm(li[3], reduced).astype(BF16))
        g_leaf[...] = g + mm(h, inc_leaf[...])
        net.arrived(odd, k_leaf, K_LEAF)
        h_leaf[...] = mm(h, k_leaf[...]).astype(BF16)

    copies[7].wait()
    copies[8].wait()
    placed = mm(no[1], hot_node).astype(BF16)
    q1[...] = placed[:, :RANK]
    uf = mm(ni[3], ni[2]).astype(BF16)
    h_node[...] = (placed[:, RANK:].astype(F32) - mm(q1[...], uf)).astype(BF16)

    @pl.when(u8 | u16)
    def _():
        ul = mm(ni[3], ni[0]).astype(BF16)
        big_g[...] = mm(q1[...], mm(ul, p1[...]).astype(BF16))

    net.arrived(u16, top, TOP)

    @pl.when(u16)
    def _():
        m_top[...] = (
            big_g[...] + mm(h_node[...], mm(top[...], s_mat[...]).astype(BF16))
        ).astype(BF16)

    m_top_left.start(m_top.at[lower], m_in)
    m_top_right.start(m_top.at[upper], m_in)

    net.arrived(n16, s_half, S_HALF)

    @pl.when(n16)
    def _():
        both_m = mm(s_half[...], s_mat[...]).astype(BF16)
        m_hub[...] = both_m[:, :RANK]
        m_out[...] = both_m[:, RANK:]

    m_to_hub.start(m_out, m_hub)

    net.arrived(lead, m_hub, M_HUB)
    net.arrived(hub, s_hub, S_HUB)

    @pl.when(hub)
    def _():
        cm[...] = mm(m_hub[...], s_hub[...]).astype(BF16)

    net.arrived(hub, hb.at[lower], HB_LEFT)
    net.arrived(hub, hb.at[upper], HB_RIGHT)

    @pl.when(hub)
    def _():
        part_own[...] = mm(cm[...], hb[...])
        skel_hub[...] = part_own[...].astype(BF16)

    for i in range(3):
        part_to_root[i].start(skel_hub, parts.at[i])

    @pl.when(hub)
    def _():
        skel_eight[...] = mm(s_hub[...], hb[...]).astype(BF16)

    n8_up.start(skel_eight, merged.at[upper])

    @pl.when(n16)
    def _():
        merged[lower] = skel_eight[...]

    net.arrived(u8, m_in, M_TOP)
    net.arrived(u8, s_other, S_OTHER)

    def four_rows(own, other, mine):
        wide = jnp.concatenate(
            [mm(m_in[:, own], s_mat[...]), mm(m_in[:, other], s_other[...])], axis=1
        ).astype(BF16)
        full = mm(h_node[...], wide)
        near = (full[:, :ROWS] + big_g[...]).astype(BF16)
        far = full[:, ROWS:].astype(BF16)
        m_rows[:, pl.ds(mine * ROWS, ROWS)] = near
        m_rows[:, pl.ds((1 - mine) * ROWS, ROWS)] = far

    @pl.when(last & (c == 3))
    def _():
        four_rows(lower, upper, 0)

    @pl.when(last & (c == 11))
    def _():
        four_rows(upper, lower, 1)

    m_four_left.start(m_rows.at[lower], m_four)
    m_four_right.start(m_rows.at[upper], m_four)

    for i in range(3):
        net.arrived(last, parts.at[i], PART_0 + i)

    @pl.when(last)
    def _():
        total = part_own[...] + parts[0].astype(F32)
        total = total + parts[1].astype(F32) + parts[2].astype(F32)
        skel_root[...] = total.astype(BF16)

    col_up.start(skel_root, merged.at[upper])

    @pl.when(col_even)
    def _():
        merged[lower] = skel_root[...]

    net.arrived(n4 | n8 | n32 | u4, merged.at[lower], B_LEFT)
    net.arrived(node, merged.at[upper], B_RIGHT)

    @pl.when(node)
    def _():
        skel_node[...] = mm(s_mat[...], merged[...]).astype(BF16)

    n2_left.start(skel_node, merged.at[lower])
    n2_right.start(skel_node, merged.at[upper])
    n4_hub_left.start(skel_node, hb.at[lower])
    n4_hub_right.start(skel_node, hb.at[upper])
    n4_left.start(skel_node, merged.at[lower])
    n4_right.start(skel_node, merged.at[upper])
    n16_left.start(skel_node, merged.at[lower])
    n16_right.start(skel_node, merged.at[upper])
    u2_left.start(skel_node, merged.at[lower])
    u2_right.start(skel_node, merged.at[upper])
    place = pl.ds(pl.multiple_of((c // 4) * RANK, RANK), RANK)
    for m in peer:
        m.start(skel_node, peers.at[place])

    @pl.when(node)
    def _():
        eliminated = mm(p1[...], merged[...]).astype(BF16)
        reduced = mm(ni[0], eliminated).astype(BF16)
        solved = mm(ni[3], reduced).astype(BF16)
        g_node[...] = mm(q1[...], solved)

    @pl.when(n8 | n32)
    def _():
        values[...] = g_node[...].astype(BF16)

    @pl.when(u4)
    def _():
        peers[place] = skel_node[...]

    for k in (1, 2, 3):
        arrival = pl.ds(pl.multiple_of(lax.rem(c // 4 + 4 - k, 4) * RANK, RANK), RANK)
        net.arrived(u4, peers.at[arrival], PEER_1 + k - 1)
    net.arrived(u4, m_four, M_FOUR)

    @pl.when(u4)
    def _():
        inc_node[...] = mm(m_four[...], peers[...]).astype(BF16)

    takes = n2 | n4 | n16 | u2
    net.arrived(takes, inc_node, INC)

    @pl.when(takes | u4)
    def _():
        values[...] = (g_node[...] + mm(h_node[...], inc_node[...])).astype(BF16)

    u4_down_left.start(values.at[lower], inc_node)
    u4_down_right.start(values.at[upper], inc_node)
    u2_down.start(values.at[upper], inc_root)
    n32_down_left.start(values.at[lower], inc_node)
    n32_down_right.start(values.at[upper], inc_node)
    n16_down.start(values.at[upper], loc_hub)
    n8_down_left.start(values.at[lower], inc_node)
    n8_down_right.start(values.at[upper], inc_node)
    n4_down_left.start(values.at[lower], inc_node)
    n4_down_right.start(values.at[upper], inc_node)
    n2_down.start(values.at[upper], inc_leaf)

    @pl.when(n16)
    def _():
        loc_hub[...] = values[lower]

    @pl.when(n2)
    def _():
        inc_leaf[...] = values[lower]

    @pl.when(u2)
    def _():
        inc_root[...] = values[lower]

    n32_k_left.start(h_node.at[lower], k_node)
    n32_k_right.start(h_node.at[upper], k_node)
    n8_k_left.start(h_node.at[lower], k_node)
    n8_k_right.start(h_node.at[upper], k_node)
    passes = n16 | n4 | n2
    net.arrived(passes, k_node, K_NODE)

    @pl.when(passes)
    def _():
        kv[...] = mm(h_node[...], k_node[...]).astype(BF16)

    n16_k.start(kv.at[upper], k_hub)
    n4_k_left.start(kv.at[lower], k_node)
    n4_k_right.start(kv.at[upper], k_node)
    n2_k.start(kv.at[upper], k_leaf)

    @pl.when(n16)
    def _():
        k_hub[...] = kv[lower]

    @pl.when(n2)
    def _():
        k_leaf[...] = kv[lower]

    copies[9].wait()
    copies[10].wait()

    @pl.when(jnp.logical_not(last))
    def _():
        leaf_down()

    net.arrived(col_odd | (hub & (x < 3)), inc_root, INC_ROOT)
    for m in root_down:
        m.start(inc_root, inc_root)
    net.arrived(lead, k_hub, K_HUB)
    net.arrived(lead, loc_hub, LOC_HUB)

    @pl.when(hub)
    def _():
        inc_hub[...] = (loc_hub[...].astype(F32) + mm(k_hub[...], inc_root[...])).astype(BF16)

    for m in hub_down:
        m.start(inc_hub, inc_hub)

    @pl.when(last)
    def _():
        leaf_down()

    net.arrived(jnp.logical_not(hub), inc_hub, INC_HUB)
    out[0, 0] = (g_leaf[...] + mm(h_leaf[...], inc_hub[...])).astype(BF16)
    net.finish()


def solution(mesh):
    vm = pltpu.VMEM
    vector = vm((RANK, RHS), BF16)
    pair = vm((ROWS, RHS), BF16)
    square = vm((RANK, RANK), BF16)
    wide = vm((RANK, ROWS), BF16)
    tall = vm((ROWS, RANK), BF16)
    scratch = [
        pair,
        vm((2, ROWS, ROWS), BF16),
        vm((4, RANK, RANK), BF16),
        vm((1, ROWS), jnp.int32),
        vm((2, ROWS, ROWS), BF16),
        vm((4, RANK, RANK), BF16),
        vm((1, ROWS), jnp.int32),
        vector,
        vector,
        pair,
        vector,
        square,
        vector,
        vector,
        pair,
        wide,
        tall,
        vm((ROWS, RHS), F32),
        tall,
        vm((ROWS, RHS), F32),
        wide,
        tall,
        pair,
        wide,
        square,
        square,
        square,
        square,
        vm((3, RANK, RHS), BF16),
        vm((RANK, RHS), F32),
        vector,
        vector,
        wide,
        vector,
        vector,
        vector,
        square,
        square,
        tall,
        vm((ROWS, ROWS), F32),
        vm((ROWS, ROWS), BF16),
        wide,
        wide,
        vm((RANK, 4 * RANK), BF16),
        vm((ROWS, 4 * RANK), BF16),
        vm((4 * RANK, RHS), BF16),
        vector,
        pltpu.SemaphoreType.DMA((11,)),
        pltpu.SemaphoreType.DMA((MESSAGES,)),
        pltpu.SemaphoreType.DMA((SLOTS,)),
    ]
    call = pl.pallas_call(
        kernel,
        out_shape=jax.ShapeDtypeStruct((1, 1, ROWS, RHS), BF16),
        in_specs=[pl.BlockSpec(memory_space=pl.ANY)] * 7,
        out_specs=pl.BlockSpec(memory_space=pltpu.VMEM),
        scratch_shapes=scratch,
        compiler_params=pltpu.CompilerParams(
            collective_id=0, has_side_effects=True, vmem_limit_bytes=62 * 1024 * 1024
        ),
        name="tree",
    )
    in_specs = (
        P("col", "row", None, None),
        P("col", "row", None, None, None),
        P("col", "row", None, None, None),
        P("col", "row", None),
        P("col", "row", None, None, None),
        P("col", "row", None, None, None),
        P("col", "row", None),
    )
    out_specs = P("col", "row", None, None)
    return jax.shard_map(call, mesh=mesh, in_specs=in_specs, out_specs=out_specs, check_vma=False)
```

```python
import functools

import jax
import jax.numpy as jnp
from jax import lax
from jax.experimental import pallas as pl
from jax.experimental.pallas import tpu as pltpu
from jax.sharding import PartitionSpec as P

MESH = pl.DeviceIdType.MESH
BF16 = jnp.bfloat16
F32 = jnp.float32
RANK = 256
ROWS = 512
RHS = 128


def mm(a, b):
    return jnp.dot(a, b, preferred_element_type=F32)


def one_hot(order_ref):
    rows = lax.broadcasted_iota(jnp.int32, (ROWS, ROWS), 0)
    return jnp.where(rows == order_ref[...], 1.0, 0.0).astype(BF16)


def gather_rows(hot, block):
    return lax.dot_general(hot, block, (((0,), (0,)), ((), ())), preferred_element_type=F32)


class Message:
    def __init__(self, net, out_cond, dst, in_cond, src, slot):
        self.net, self.out_cond, self.dst, self.in_cond, self.src = net, out_cond, dst, in_cond, src
        self.slot, self.lane = slot, len(net.messages)
        net.messages.append(self)

    def start(self, src_ref, dst_ref):
        self.copy = pltpu.make_async_remote_copy(
            src_ref=src_ref,
            dst_ref=dst_ref,
            send_sem=self.net.send_sem.at[self.lane],
            recv_sem=self.net.recv_sem.at[self.slot],
            device_id=self.dst,
            device_id_type=MESH,
        )
        pl.when(self.out_cond)(self.copy.start)

    def finish(self):
        pl.when(self.out_cond)(self.copy.wait_send)


class Net:
    def __init__(self, send_sem, recv_sem):
        self.messages, self.send_sem, self.recv_sem = [], send_sem, recv_sem
        c = lax.axis_index("col")
        self.partner = (lax.axis_index("row"), c + 1 - 2 * lax.rem(c, 2))

    def add(self, out_cond, dst, in_cond, src, slot):
        return Message(self, out_cond, dst, in_cond, src, slot)

    def greet(self):
        barrier = pltpu.get_barrier_semaphore()
        for m in self.messages:

            @pl.when(m.in_cond)
            def _(m=m):
                pl.semaphore_signal(barrier, inc=1, device_id=m.src, device_id_type=MESH)

    def meet(self):
        count = sum(jnp.where(m.out_cond, 1, 0) for m in self.messages)
        pl.semaphore_wait(pltpu.get_barrier_semaphore(), count)

    def arrived(self, cond, ref, slot):
        copy = pltpu.make_async_remote_copy(
            src_ref=ref,
            dst_ref=ref,
            send_sem=self.send_sem.at[0],
            recv_sem=self.recv_sem.at[slot],
            device_id=self.partner,
            device_id_type=MESH,
        )
        pl.when(cond)(copy.wait_recv)

    def finish(self):
        for m in self.messages:
            m.finish()


MESSAGES = 80
(
    B_LEFT,
    B_RIGHT,
    INC,
    INC_LEAF,
    TOP,
    HB_LEFT,
    HB_RIGHT,
    S_HUB,
    M_HUB,
    S_HALF,
    K_HUB,
    PART_0,
    PART_1,
    PART_2,
    LOC_HUB,
    INC_ROOT,
    INC_HUB,
    K_NODE,
    K_LEAF,
    M_TOP,
    S_OTHER,
    M_FOUR,
    M_FOUR_LATE,
    PEER_1,
    PEER_2,
    PEER_3,
    S_LATE_0,
    S_LATE_1,
    LATE_0,
    LATE_1,
    LATE_2,
    LATE_3,
) = range(32)
SLOTS = 32


def kernel(
    rhs_h, lo_h, li_h, lord_h, no_h, ni_h, nord_h, out,
    rhs, lo, li, lord, no, ni, nord,
    leaf_reduced, skel_leaf, merged, skel_node, top, inc_node, inc_leaf, values,
    s_mat, h_node, g_node, h_leaf, g_leaf, p1, q1,
    hb, s_hub, m_hub, m_out, s_half, k_hub, parts, part_own, skel_hub, skel_eight, cm, loc_hub,
    inc_root, inc_hub, k_node, k_leaf, kv, big_g, m_top, m_in, s_other, m_map, m_rows, peers, skel_root, s_late, late, m_late,
    load_sem, send_sem, recv_sem,
):
    r = lax.axis_index("row")
    c = lax.axis_index("col")
    x = r // 8
    y = lax.rem(r, 8)
    even = lax.rem(y, 2) == 0
    odd = jnp.logical_not(even)
    n2 = even
    n4 = (y == 1) | (y == 5)
    n8 = y == 3
    hub = y == 7
    n16 = hub & ((x == 0) | (x == 2))
    n32 = hub & (x == 1)
    last = hub & (x == 3)
    col_even = last & (lax.rem(c, 2) == 0)
    col_odd = last & (lax.rem(c, 2) == 1)
    u2 = col_even
    u4 = last & (lax.rem(c, 4) == 1)
    u8 = last & (lax.rem(c, 8) == 3)
    u16 = last & (c == 7)
    block = last & (c == 15)
    node = jnp.logical_not(u8 | u16 | block)
    lead = hub & jnp.logical_not(n16)

    loads = [
        (ni_h.at[0, 0, pl.ds(0, 2)], ni.at[pl.ds(0, 2)]),
        (lord_h.at[0], lord),
        (lo_h.at[0, 0, 0], lo.at[0]),
        (rhs_h.at[0, 0], rhs),
        (li_h.at[0, 0, pl.ds(0, 2)], li.at[pl.ds(0, 2)]),
        (nord_h.at[0], nord),
        (no_h.at[0, 0, 0], no.at[0]),
        (no_h.at[0, 0, 1], no.at[1]),
        (ni_h.at[0, 0, pl.ds(2, 2)], ni.at[pl.ds(2, 2)]),
        (lo_h.at[0, 0, 1], lo.at[1]),
        (li_h.at[0, 0, pl.ds(2, 2)], li.at[pl.ds(2, 2)]),
    ]
    copies = [
        pltpu.make_async_copy(src, dst, load_sem.at[i]) for i, (src, dst) in enumerate(loads)
    ]
    for copy in copies:
        copy.start()

    net = Net(send_sem, recv_sem)
    add = net.add
    leaf_up = add(odd, (r - 1, c), even, (r + 1, c), B_RIGHT)
    n2_left = add((y == 0) | (y == 4), (r + 1, c), n4, (r - 1, c), B_LEFT)
    n2_right = add((y == 2) | (y == 6), (r - 1, c), n4, (r + 1, c), B_RIGHT)
    n4_hub_left = add(y == 1, (r + 6, c), hub, (r - 6, c), HB_LEFT)
    n4_hub_right = add(y == 5, (r + 2, c), hub, (r - 2, c), HB_RIGHT)
    n4_left = add(y == 1, (r + 2, c), n8, (r - 2, c), B_LEFT)
    n4_right = add(y == 5, (r - 2, c), n8, (r + 2, c), B_RIGHT)
    s_to_hub = add(n8, (r + 4, c), hub, (r - 4, c), S_HUB)
    s_left = add(n32, (r - 8, c), hub & (x == 0), (r + 8, c), S_HALF)
    s_right = add(n32, (r + 8, c), hub & (x == 2), (r - 8, c), S_HALF)
    m_to_hub = add(n16, (r + 8, c), lead, (r - 8, c), M_HUB)
    part_to_root = [
        add(hub & (x == i), (31, c), last, (8 * i + 7, c), PART_0 + i) for i in range(3)
    ]
    n8_up = add(lead, (r - 8, c), n16, (r + 8, c), B_RIGHT)
    n16_left = add(hub & (x == 0), (r + 8, c), n32, (r - 8, c), B_LEFT)
    n16_right = add(hub & (x == 2), (r - 8, c), n32, (r + 8, c), B_RIGHT)
    col_up = add(col_odd, (r, c - 1), col_even, (r, c + 1), B_RIGHT)
    u2_left = add(last & (lax.rem(c, 4) == 0), (r, c + 1), u4, (r, c - 1), B_LEFT)
    u2_right = add(last & (lax.rem(c, 4) == 2), (r, c - 1), u4, (r, c + 1), B_RIGHT)
    early4 = last & ((c == 1) | (c == 5))
    late4 = last & ((c == 9) | (c == 13))
    direct = {
        d: [add(last & (c == p), (r, d), last & (c == d), (r, p), LATE_0 + i) for i, p in enumerate((8, 10, 12, 14))]
        for d in (1, 5)
    }
    s_direct = [
        add(last & (c == p), (r, d), last & (c == d), (r, p), S_LATE_0 + i)
        for i, p in enumerate((9, 13))
        for d in (1, 5)
    ]

    def among(sources, k):
        out = functools.reduce(jnp.logical_or, [c == p for p in sources])
        into = functools.reduce(jnp.logical_or, [c == (p + 4 * k) % 16 for p in sources])
        return add(last & out, (r, lax.rem(c + 4 * k, 16)), last & into, (r, lax.rem(c + 16 - 4 * k, 16)), PEER_1 + k - 1)

    peer = [among((1, 5), 2), among((1, 5, 9), 1), among((1, 5, 13), 3)]
    top_send = add(block, (r, c - 8), u16, (r, c + 8), TOP)
    m_top_left = add(u16, (r, c - 4), last & (c == 3), (r, c + 4), M_TOP)
    m_top_right = add(u16, (r, c + 4), last & (c == 11), (r, c - 4), M_TOP)
    s_exchange = add(u8, (r, lax.rem(c + 8, 16)), u8, (r, lax.rem(c + 8, 16)), S_OTHER)
    m_four = [
        add(u8, (r, c - 2), last & (lax.rem(c, 8) == 1), (r, c + 2), slot)
        for slot in (M_FOUR_LATE, M_FOUR)
    ] + [
        add(u8, (r, c + 2), last & (lax.rem(c, 8) == 5), (r, c - 2), slot)
        for slot in (M_FOUR_LATE, M_FOUR)
    ]
    n32_down_left = add(n32, (r - 8, c), hub & (x == 0), (r + 8, c), INC)
    n32_down_right = add(n32, (r + 8, c), hub & (x == 2), (r - 8, c), INC)
    n16_down = add(n16, (r + 8, c), lead, (r - 8, c), LOC_HUB)
    n8_down_left = add(n8, (r - 2, c), y == 1, (r + 2, c), INC)
    n8_down_right = add(n8, (r + 2, c), y == 5, (r - 2, c), INC)
    n4_down_left = add(n4, (r - 1, c), (y == 0) | (y == 4), (r + 1, c), INC)
    n4_down_right = add(n4, (r + 1, c), (y == 2) | (y == 6), (r - 1, c), INC)
    n2_down = add(n2, (r + 1, c), odd, (r - 1, c), INC_LEAF)
    u4_down_left = add(u4, (r, c - 1), last & (lax.rem(c, 4) == 0), (r, c + 1), INC)
    u4_down_right = add(u4, (r, c + 1), last & (lax.rem(c, 4) == 2), (r, c - 1), INC)
    u2_down = add(u2, (r, c + 1), col_odd, (r, c - 1), INC_ROOT)
    n32_k_left = add(n32, (r - 8, c), hub & (x == 0), (r + 8, c), K_NODE)
    n32_k_right = add(n32, (r + 8, c), hub & (x == 2), (r - 8, c), K_NODE)
    n16_k = add(n16, (r + 8, c), lead, (r - 8, c), K_HUB)
    n8_k_left = add(n8, (r - 2, c), y == 1, (r + 2, c), K_NODE)
    n8_k_right = add(n8, (r + 2, c), y == 5, (r - 2, c), K_NODE)
    n4_k_left = add(n4, (r - 1, c), (y == 0) | (y == 4), (r + 1, c), K_NODE)
    n4_k_right = add(n4, (r + 1, c), (y == 2) | (y == 6), (r - 1, c), K_NODE)
    n2_k = add(n2, (r + 1, c), odd, (r - 1, c), K_LEAF)
    root_down = [add(last, (8 * i + 7, c), hub & (x == i), (31, c), INC_ROOT) for i in (1, 0, 2)]
    hub_down = [
        add(hub, (8 * x + i, c), y == i, (8 * x + 7, c), INC_HUB) for i in (0, 3, 1, 6, 2, 5, 4)
    ]
    net.greet()

    lower = pl.ds(0, RANK)
    upper = pl.ds(RANK, RANK)
    near = pl.ds(0, ROWS)
    far = pl.ds(ROWS, ROWS)

    @pl.when(block)
    def _():
        net.meet()

    copies[0].wait()
    top_send.start(ni.at[0], top)

    copies[1].wait()
    hot_leaf = one_hot(lord)
    copies[2].wait()
    copies[3].wait()
    rotated = mm(lo[0], rhs[...])
    high = rotated.astype(BF16)
    low = (rotated - high.astype(F32)).astype(BF16)
    both = gather_rows(hot_leaf, jnp.concatenate([high, low], axis=1))
    rotated = both[:, :RHS] + both[:, RHS:]
    copies[4].wait()
    leaf_reduced[...] = mm(li[0], rotated[:RANK].astype(BF16)).astype(BF16)
    skel_leaf[...] = (rotated[RANK:] - mm(li[1], leaf_reduced[...])).astype(BF16)

    @pl.when(jnp.logical_not(block))
    def _():
        net.meet()

    leaf_up.start(skel_leaf, merged.at[upper])

    @pl.when(even)
    def _():
        merged[lower] = skel_leaf[...]

    copies[5].wait()
    hot_node = one_hot(nord)
    copies[6].wait()
    gathered = gather_rows(hot_node, no[0])
    p1[...] = gathered[:RANK].astype(BF16)
    el = mm(ni[1], ni[0]).astype(BF16)
    s_mat[...] = (gathered[RANK:] - mm(el, p1[...])).astype(BF16)
    s_to_hub.start(s_mat, s_hub)
    s_left.start(s_mat.at[:, lower], s_half)
    s_right.start(s_mat.at[:, upper], s_half)
    s_exchange.start(s_mat, s_other)
    for i, m in enumerate(s_direct):
        m.start(s_mat, s_late.at[i // 2])

    def leaf_down():
        placed = mm(lo[1], one_hot(lord)).astype(BF16)
        first = placed[:, :RANK]
        uf = mm(li[3], li[2]).astype(BF16)
        h = (placed[:, RANK:].astype(F32) - mm(first, uf)).astype(BF16)
        reduced = leaf_reduced[...]
        net.arrived(odd, inc_leaf, INC_LEAF)
        g = mm(first, mm(li[3], reduced).astype(BF16))
        g_leaf[...] = g + mm(h, inc_leaf[...])
        net.arrived(odd, k_leaf, K_LEAF)
        h_leaf[...] = mm(h, k_leaf[...]).astype(BF16)

    copies[7].wait()
    copies[8].wait()
    placed = mm(no[1], hot_node).astype(BF16)
    q1[...] = placed[:, :RANK]
    uf = mm(ni[3], ni[2]).astype(BF16)
    h_node[...] = (placed[:, RANK:].astype(F32) - mm(q1[...], uf)).astype(BF16)

    @pl.when(u8 | u16)
    def _():
        ul = mm(ni[3], ni[0]).astype(BF16)
        big_g[...] = mm(q1[...], mm(ul, p1[...]).astype(BF16))

    net.arrived(u16, top, TOP)

    @pl.when(u16)
    def _():
        m_top[...] = (
            big_g[...] + mm(h_node[...], mm(top[...], s_mat[...]).astype(BF16))
        ).astype(BF16)

    m_top_left.start(m_top.at[lower], m_in)
    m_top_right.start(m_top.at[upper], m_in)

    net.arrived(n16, s_half, S_HALF)

    @pl.when(n16)
    def _():
        both_m = mm(s_half[...], s_mat[...]).astype(BF16)
        m_hub[...] = both_m[:, :RANK]
        m_out[...] = both_m[:, RANK:]

    m_to_hub.start(m_out, m_hub)

    net.arrived(lead, m_hub, M_HUB)
    net.arrived(hub, s_hub, S_HUB)

    @pl.when(hub)
    def _():
        cm[...] = mm(m_hub[...], s_hub[...]).astype(BF16)

    net.arrived(hub, hb.at[lower], HB_LEFT)
    net.arrived(hub, hb.at[upper], HB_RIGHT)

    @pl.when(hub)
    def _():
        part_own[...] = mm(cm[...], hb[...])
        skel_hub[...] = part_own[...].astype(BF16)

    for i in range(3):
        part_to_root[i].start(skel_hub, parts.at[i])

    @pl.when(hub)
    def _():
        skel_eight[...] = mm(s_hub[...], hb[...]).astype(BF16)

    n8_up.start(skel_eight, merged.at[upper])

    @pl.when(n16)
    def _():
        merged[lower] = skel_eight[...]

    net.arrived(u8, m_in, M_TOP)
    net.arrived(u8, s_other, S_OTHER)

    def four_rows(own, other, mine):
        wide = jnp.concatenate(
            [mm(m_in[:, own], s_mat[...]), mm(m_in[:, other], s_other[...])], axis=1
        ).astype(BF16)
        full = mm(h_node[...], wide)
        m_rows[:, pl.ds(mine * ROWS, ROWS)] = (full[:, :ROWS] + big_g[...]).astype(BF16)
        m_rows[:, pl.ds((1 - mine) * ROWS, ROWS)] = full[:, ROWS:].astype(BF16)

    @pl.when(last & (c == 3))
    def _():
        four_rows(lower, upper, 0)

    @pl.when(last & (c == 11))
    def _():
        four_rows(upper, lower, 1)

    for m, child, cols in zip(m_four, (lower, lower, upper, upper), (far, near) * 2):
        m.start(m_rows.at[child, cols], m_map.at[:, cols])

    for i in range(3):
        net.arrived(last, parts.at[i], PART_0 + i)

    @pl.when(last)
    def _():
        total = part_own[...] + parts[0].astype(F32)
        total = total + parts[1].astype(F32) + parts[2].astype(F32)
        skel_root[...] = total.astype(BF16)

    col_up.start(skel_root, merged.at[upper])

    @pl.when(col_even)
    def _():
        merged[lower] = skel_root[...]

    net.arrived(n4 | n8 | n32 | u4, merged.at[lower], B_LEFT)
    net.arrived(node, merged.at[upper], B_RIGHT)

    @pl.when(node)
    def _():
        skel_node[...] = mm(s_mat[...], merged[...]).astype(BF16)

    n2_left.start(skel_node, merged.at[lower])
    n2_right.start(skel_node, merged.at[upper])
    n4_hub_left.start(skel_node, hb.at[lower])
    n4_hub_right.start(skel_node, hb.at[upper])
    n4_left.start(skel_node, merged.at[lower])
    n4_right.start(skel_node, merged.at[upper])
    n16_left.start(skel_node, merged.at[lower])
    n16_right.start(skel_node, merged.at[upper])
    for i, m in enumerate(direct[1]):
        m.start(skel_node, late.at[pl.ds(i * RANK, RANK)])
    u2_left.start(skel_node, merged.at[lower])
    u2_right.start(skel_node, merged.at[upper])
    for i, m in enumerate(direct[5]):
        m.start(skel_node, late.at[pl.ds(i * RANK, RANK)])
    place = pl.ds(pl.multiple_of((c // 4) * RANK, RANK), RANK)
    for m in peer:
        m.start(skel_node, peers.at[place])

    @pl.when(node)
    def _():
        eliminated = mm(p1[...], merged[...]).astype(BF16)
        reduced = mm(ni[0], eliminated).astype(BF16)
        solved = mm(ni[3], reduced).astype(BF16)
        g_node[...] = mm(q1[...], solved)

    @pl.when(n8 | n32)
    def _():
        values[...] = g_node[...].astype(BF16)

    @pl.when(u4)
    def _():
        peers[place] = skel_node[...]

    net.arrived(u4, m_map.at[:, far], M_FOUR_LATE)
    for i in range(2):
        net.arrived(early4, s_late.at[i], S_LATE_0 + i)

    @pl.when(early4)
    def _():
        for i in range(2):
            m_late[:, pl.ds(i * ROWS, ROWS)] = mm(
                m_map[:, pl.ds(ROWS + i * RANK, RANK)], s_late[i]
            ).astype(BF16)

    net.arrived(u4, m_map.at[:, near], M_FOUR)
    takes_from = {1: (5, 9, 13), 2: (9, 13), 3: (1, 9, 13)}
    for k in (1, 2, 3):
        arrival = pl.ds(pl.multiple_of(lax.rem(c // 4 + 4 - k, 4) * RANK, RANK), RANK)
        cond = functools.reduce(jnp.logical_or, [c == p for p in takes_from[k]])
        net.arrived(last & cond, peers.at[arrival], PEER_1 + k - 1)

    @pl.when(late4)
    def _():
        inc_node[...] = mm(m_map[...], peers[...]).astype(BF16)

    @pl.when(early4)
    def _():
        part_own[...] = mm(m_map[:, near], peers[near])

    for i in range(4):
        net.arrived(early4, late.at[pl.ds(i * RANK, RANK)], LATE_0 + i)

    @pl.when(early4)
    def _():
        inc_node[...] = (part_own[...] + mm(m_late[...], late[...])).astype(BF16)

    takes = n2 | n4 | n16 | u2
    net.arrived(takes, inc_node, INC)

    @pl.when(takes | u4)
    def _():
        values[...] = (g_node[...] + mm(h_node[...], inc_node[...])).astype(BF16)

    u4_down_left.start(values.at[lower], inc_node)
    u4_down_right.start(values.at[upper], inc_node)
    u2_down.start(values.at[upper], inc_root)
    n32_down_left.start(values.at[lower], inc_node)
    n32_down_right.start(values.at[upper], inc_node)
    n16_down.start(values.at[upper], loc_hub)
    n8_down_left.start(values.at[lower], inc_node)
    n8_down_right.start(values.at[upper], inc_node)
    n4_down_left.start(values.at[lower], inc_node)
    n4_down_right.start(values.at[upper], inc_node)
    n2_down.start(values.at[upper], inc_leaf)

    @pl.when(n16)
    def _():
        loc_hub[...] = values[lower]

    @pl.when(n2)
    def _():
        inc_leaf[...] = values[lower]

    @pl.when(u2)
    def _():
        inc_root[...] = values[lower]

    n32_k_left.start(h_node.at[lower], k_node)
    n32_k_right.start(h_node.at[upper], k_node)
    n8_k_left.start(h_node.at[lower], k_node)
    n8_k_right.start(h_node.at[upper], k_node)
    passes = n16 | n4 | n2
    net.arrived(passes, k_node, K_NODE)

    @pl.when(passes)
    def _():
        kv[...] = mm(h_node[...], k_node[...]).astype(BF16)

    n16_k.start(kv.at[upper], k_hub)
    n4_k_left.start(kv.at[lower], k_node)
    n4_k_right.start(kv.at[upper], k_node)
    n2_k.start(kv.at[upper], k_leaf)

    @pl.when(n16)
    def _():
        k_hub[...] = kv[lower]

    @pl.when(n2)
    def _():
        k_leaf[...] = kv[lower]

    copies[9].wait()
    copies[10].wait()

    @pl.when(jnp.logical_not(last))
    def _():
        leaf_down()

    net.arrived(col_odd | (hub & (x < 3)), inc_root, INC_ROOT)
    for m in root_down:
        m.start(inc_root, inc_root)
    net.arrived(lead, k_hub, K_HUB)
    net.arrived(lead, loc_hub, LOC_HUB)

    @pl.when(hub)
    def _():
        inc_hub[...] = (loc_hub[...].astype(F32) + mm(k_hub[...], inc_root[...])).astype(BF16)

    for m in hub_down:
        m.start(inc_hub, inc_hub)

    @pl.when(last)
    def _():
        leaf_down()

    net.arrived(jnp.logical_not(hub), inc_hub, INC_HUB)
    out[0, 0] = (g_leaf[...] + mm(h_leaf[...], inc_hub[...])).astype(BF16)
    net.finish()


def solution(mesh):
    vm = pltpu.VMEM
    vector = vm((RANK, RHS), BF16)
    pair = vm((ROWS, RHS), BF16)
    square = vm((RANK, RANK), BF16)
    wide = vm((RANK, ROWS), BF16)
    tall = vm((ROWS, RANK), BF16)
    scratch = [
        pair,
        vm((2, ROWS, ROWS), BF16),
        vm((4, RANK, RANK), BF16),
        vm((1, ROWS), jnp.int32),
        vm((2, ROWS, ROWS), BF16),
        vm((4, RANK, RANK), BF16),
        vm((1, ROWS), jnp.int32),
        vector,
        vector,
        pair,
        vector,
        square,
        vector,
        vector,
        pair,
        wide,
        tall,
        vm((ROWS, RHS), F32),
        tall,
        vm((ROWS, RHS), F32),
        wide,
        tall,
        pair,
        wide,
        square,
        square,
        square,
        square,
        vm((3, RANK, RHS), BF16),
        vm((RANK, RHS), F32),
        vector,
        vector,
        wide,
        vector,
        vector,
        vector,
        square,
        square,
        tall,
        vm((ROWS, ROWS), F32),
        vm((ROWS, ROWS), BF16),
        wide,
        wide,
        vm((RANK, 4 * RANK), BF16),
        vm((ROWS, 4 * RANK), BF16),
        vm((4 * RANK, RHS), BF16),
        vector,
        vm((2, RANK, ROWS), BF16),
        vm((4 * RANK, RHS), BF16),
        vm((RANK, 4 * RANK), BF16),
        pltpu.SemaphoreType.DMA((11,)),
        pltpu.SemaphoreType.DMA((MESSAGES,)),
        pltpu.SemaphoreType.DMA((SLOTS,)),
    ]
    call = pl.pallas_call(
        kernel,
        out_shape=jax.ShapeDtypeStruct((1, 1, ROWS, RHS), BF16),
        in_specs=[pl.BlockSpec(memory_space=pltpu.HBM)] * 7,
        out_specs=pl.BlockSpec(memory_space=pltpu.VMEM),
        scratch_shapes=scratch,
        compiler_params=pltpu.CompilerParams(
            collective_id=0, has_side_effects=True, vmem_limit_bytes=40 * 1024 * 1024
        ),
        name="tree",
    )

    def local(*args):
        return call(*[pltpu.with_memory_space_constraint(a, pltpu.HBM) for a in args])

    in_specs = (
        P("col", "row", None, None),
        P("col", "row", None, None, None),
        P("col", "row", None, None, None),
        P("col", "row", None),
        P("col", "row", None, None, None),
        P("col", "row", None, None, None),
        P("col", "row", None),
    )
    out_specs = P("col", "row", None, None)
    return jax.shard_map(local, mesh=mesh, in_specs=in_specs, out_specs=out_specs, check_vma=False)
```

```python
import functools

import jax
import jax.numpy as jnp
from jax import lax
from jax.experimental import pallas as pl
from jax.experimental.pallas import tpu as pltpu
from jax.sharding import PartitionSpec as P

MESH = pl.DeviceIdType.MESH
BF16 = jnp.bfloat16
F32 = jnp.float32
RANK = 256
ROWS = 512
RHS = 128
PARTS = 2
CUT = RHS // PARTS


def mm(a, b):
    return jnp.dot(a, b, preferred_element_type=F32)


def nt(a, b):
    return lax.dot_general(a, b, (((1,), (1,)), ((), ())), preferred_element_type=F32)


def tn(a, b):
    return lax.dot_general(a, b, (((0,), (0,)), ((), ())), preferred_element_type=F32)


def one_hot(order_ref):
    rows = lax.broadcasted_iota(jnp.int32, (ROWS, ROWS), 0)
    return jnp.where(rows == order_ref[...], 1.0, 0.0).astype(BF16)


def any_of(value, choices):
    return functools.reduce(jnp.logical_or, [value == p for p in choices])


VECTORS = (
    "left", "right", "inc", "inc_leaf", "hb_left", "hb_right", "part0", "part1", "part2",
    "loc_hub", "inc_root", "inc_hub", "peer0", "peer1", "peer2", "peer3", "late0",
    "late1", "late2", "late3",
)
MATRICES = (
    "top", "s_hub", "m_hub", "s_half", "k_hub", "k_node", "k_leaf", "m_top", "s_other",
    "m_near", "m_far", "s_late0", "s_late1",
)
SLOT = {name: PARTS * i for i, name in enumerate(VECTORS)}
SLOT.update({name: PARTS * len(VECTORS) + i for i, name in enumerate(MATRICES)})
SLOTS = PARTS * len(VECTORS) + len(MATRICES)
LANES = 120
ANY, HUB, LAST = range(3)


def rows_of(part):
    return pl.ds(part * CUT, CUT)


def slab(index, part=None):
    start, size = index * RHS, RHS
    if part is not None:
        start, size = start + part * CUT, CUT
    if not isinstance(index, int):
        start = pl.multiple_of(start, CUT)
    return pl.ds(start, size)


def piece(ref, part):
    if isinstance(ref, tuple):
        return ref[0].at[slab(ref[1], part)]
    return ref.at[rows_of(part)]


class Message:
    def __init__(self, net, out, dst, into, src, slot, out_zone, in_zone, like):
        self.net, self.out, self.dst, self.into, self.src = net, out, dst, into, src
        self.slot, self.out_zone, self.in_zone = slot, out_zone, in_zone
        self.wide = slot in VECTORS
        if like is None:
            self.lane = net.lanes
            net.lanes += PARTS if self.wide else 1
        else:
            self.lane = like.lane
        self.copies = []
        net.messages.append(self)

    def start(self, src_ref, dst_ref, part=None):
        shift = 0
        if self.wide:
            src_ref, dst_ref, shift = piece(src_ref, part), piece(dst_ref, part), part
        copy = pltpu.make_async_remote_copy(
            src_ref=src_ref,
            dst_ref=dst_ref,
            send_sem=self.net.send_sem.at[self.lane + shift],
            recv_sem=self.net.recv_sem.at[SLOT[self.slot] + shift],
            device_id=self.dst,
            device_id_type=MESH,
        )
        self.copies.append(copy)
        pl.when(self.out)(copy.start)

    def finish(self):
        @pl.when(self.out)
        def _():
            for copy in self.copies:
                copy.wait_send()


class Net:
    def __init__(self, send_sem, recv_sem):
        self.messages, self.lanes = [], 0
        self.send_sem, self.recv_sem = send_sem, recv_sem
        c = lax.axis_index("col")
        self.partner = (lax.axis_index("row"), c + 1 - 2 * lax.rem(c, 2))

    def add(self, out, dst, into, src, slot, out_zone=ANY, in_zone=ANY, like=None):
        return Message(self, out, dst, into, src, slot, out_zone, in_zone, like)

    def by_zone(self, zone_of, act):
        def run(zone):
            for m in self.messages:
                if zone_of(m) == zone:
                    act(m)

        run(ANY)
        run(HUB)
        run(LAST)

    def greet(self):
        barrier = pltpu.get_barrier_semaphore()

        def act(m):
            @pl.when(m.into)
            def _():
                pl.semaphore_signal(barrier, inc=1, device_id=m.src, device_id_type=MESH)

        self.by_zone(lambda m: m.in_zone, act)
        self.count = sum(m.out.astype(jnp.int32) for m in self.messages)

    def meet(self):
        pl.semaphore_wait(pltpu.get_barrier_semaphore(), self.count)

    def arrived(self, cond, ref, slot, part=None):
        shift = 0
        if slot in VECTORS:
            ref, shift = piece(ref, part), part
        copy = pltpu.make_async_remote_copy(
            src_ref=ref,
            dst_ref=ref,
            send_sem=self.send_sem.at[0],
            recv_sem=self.recv_sem.at[SLOT[slot] + shift],
            device_id=self.partner,
            device_id_type=MESH,
        )
        pl.when(cond)(copy.wait_recv)

    def finish(self, messages):
        for m in messages:
            m.finish()


def kernel(
    rhs_h, lo_h, li_h, lord_h, no_h, ni_h, nord_h, out,
    rhs, lo, li, lord, no, ni, nord,
    elim_leaf, skel_leaf, merged, skel_node, top, inc_node, inc_leaf, values,
    s_t, h_node, g_node, h_leaf, g_leaf, p1_t, q1,
    hb, s_hub, m_hub, m_out, s_half, k_hub, parts, part_own, skel_hub, skel_eight, cm_t, loc_hub,
    inc_root, inc_hub, k_node, k_leaf, kv, big_g, m_top, m_in, s_other, m_map, m_rows, peers,
    s_late, late, m_late, part_near, skel_root,
    load_sem, send_sem, recv_sem,
):
    r = lax.axis_index("row")
    c = lax.axis_index("col")
    x = r // 8
    y = lax.rem(r, 8)
    parity = lax.rem(c, 2)
    even = lax.rem(y, 2) == 0
    odd = jnp.logical_not(even)
    n2 = even
    n4 = (y == 1) | (y == 5)
    n8 = y == 3
    hub = y == 7
    low = jnp.logical_not(hub)
    x0, x1, x2 = hub & (x == 0), hub & (x == 1), hub & (x == 2)
    n16 = x0 | x2
    n32 = x1
    last = hub & (x == 3)
    lead = x1 | last
    u2 = last & (parity == 0)
    col_odd = last & (parity == 1)
    u4 = last & (lax.rem(c, 4) == 1)
    u8 = last & (lax.rem(c, 8) == 3)
    u16 = last & (c == 7)
    block = last & (c == 15)
    early4 = last & ((c == 1) | (c == 5))
    late4 = last & ((c == 9) | (c == 13))
    node = low | n16 | n32 | u2 | u4

    loads = [
        (lo_h.at[0, 0, 0], lo.at[0]),
        (rhs_h.at[0, 0], rhs),
        (lord_h.at[0], lord),
        (li_h.at[0, 0, pl.ds(0, 2)], li.at[pl.ds(0, 2)]),
        (ni_h.at[0, 0, pl.ds(0, 2)], ni.at[pl.ds(0, 2)]),
        (nord_h.at[0], nord),
        (no_h.at[0, 0, 0], no.at[0]),
        (no_h.at[0, 0, 1], no.at[1]),
        (ni_h.at[0, 0, pl.ds(2, 2)], ni.at[pl.ds(2, 2)]),
        (lo_h.at[0, 0, 1], lo.at[1]),
        (li_h.at[0, 0, pl.ds(2, 2)], li.at[pl.ds(2, 2)]),
    ]
    copies = [
        pltpu.make_async_copy(src, dst, load_sem.at[i]) for i, (src, dst) in enumerate(loads)
    ]
    for copy in copies[:7]:
        copy.start()

    net = Net(send_sem, recv_sem)
    add = net.add
    leaf_up = add(odd, (r - 1, c), even, (r + 1, c), "right")
    n2_left = add((y == 0) | (y == 4), (r + 1, c), n4, (r - 1, c), "left")
    n2_right = add((y == 2) | (y == 6), (r - 1, c), n4, (r + 1, c), "right", like=n2_left)
    n4_hub_left = add(y == 1, (r + 6, c), hub, (r - 6, c), "hb_left", ANY, HUB)
    n4_hub_right = add(y == 5, (r + 2, c), hub, (r - 2, c), "hb_right", ANY, HUB, n4_hub_left)
    n4_left = add(y == 1, (r + 2, c), n8, (r - 2, c), "left")
    n4_right = add(y == 5, (r - 2, c), n8, (r + 2, c), "right", like=n4_left)
    s_to_hub = add(n8, (r + 4, c), hub, (r - 4, c), "s_hub", ANY, HUB)
    s_left = add(x1, (r - 8, c), x0, (r + 8, c), "s_half", HUB, HUB)
    s_right = add(x1, (r + 8, c), x2, (r - 8, c), "s_half", HUB, HUB)
    m_to_hub = add(n16, (r + 8, c), lead, (r - 8, c), "m_hub", HUB, HUB)
    part_up = [
        add(hub & (x == i), (31, c), last, (8 * i + 7, c), f"part{i}", HUB, LAST) for i in range(3)
    ]
    col_up = add(col_odd, (r, c - 1), u2, (r, c + 1), "right", LAST, LAST)
    n8_up = add(lead, (r - 8, c), n16, (r + 8, c), "right", HUB, HUB)
    n16_left = add(x0, (r + 8, c), n32, (r - 8, c), "left", HUB, HUB)
    n16_right = add(x2, (r - 8, c), n32, (r + 8, c), "right", HUB, HUB, n16_left)
    u2_left = add(last & (lax.rem(c, 4) == 0), (r, c + 1), u4, (r, c - 1), "left", LAST, LAST)
    u2_right = add(last & (lax.rem(c, 4) == 2), (r, c - 1), u4, (r, c + 1), "right", LAST, LAST)

    def chosen(sources, dst, into, src, slot, like=None):
        out, into = last & any_of(c, sources), last & any_of(c, into)
        return add(out, dst, into, src, slot, LAST, LAST, like)

    direct = {1: [], 5: []}
    for d, ms in direct.items():
        for i, p in enumerate((8, 10, 12, 14)):
            ms.append(chosen((p,), (r, d), (d,), (r, p), f"late{i}", ms[0] if ms else None))
    s_direct = [
        chosen((p,), (r, d), (d,), (r, p), f"s_late{i}") for i, p in enumerate((9, 13)) for d in (1, 5)
    ]
    peer = []
    for p, others in ((1, (9, 5, 13)), (5, (13, 1, 9)), (9, (13,)), (13, (9,))):
        for n, d in enumerate(others):
            like = peer[n] if p > 1 else None
            peer.append(chosen((p,), (r, d), (d,), (r, p), f"peer{p // 4}", like))
            peer[-1].index = p // 4
    top_send = chosen((15,), (r, c - 8), (7,), (r, c + 8), "top")
    m_top_left = chosen((7,), (r, c - 4), (3,), (r, c + 4), "m_top")
    m_top_right = chosen((7,), (r, c + 4), (11,), (r, c - 4), "m_top")
    s_exchange = chosen(
        (3, 11), (r, lax.rem(c + 8, 16)), (3, 11), (r, lax.rem(c + 8, 16)), "s_other"
    )
    m_left = {n: chosen((3, 11), (r, c - 2), (1, 9), (r, c + 2), n) for n in ("m_far", "m_near")}
    m_right = {n: chosen((3, 11), (r, c + 2), (5, 13), (r, c - 2), n) for n in ("m_far", "m_near")}
    n32_down_left = add(n32, (r - 8, c), x0, (r + 8, c), "inc", HUB, HUB)
    n32_down_right = add(n32, (r + 8, c), x2, (r - 8, c), "inc", HUB, HUB)
    n16_down = add(n16, (r + 8, c), lead, (r - 8, c), "loc_hub", HUB, HUB)
    n8_down_left = add(n8, (r - 2, c), y == 1, (r + 2, c), "inc")
    n8_down_right = add(n8, (r + 2, c), y == 5, (r - 2, c), "inc")
    n4_down_left = add(n4, (r - 1, c), (y == 0) | (y == 4), (r + 1, c), "inc")
    n4_down_right = add(n4, (r + 1, c), (y == 2) | (y == 6), (r - 1, c), "inc")
    n2_down = add(n2, (r + 1, c), odd, (r - 1, c), "inc_leaf")
    u4_down_left = add(u4, (r, c - 1), last & (lax.rem(c, 4) == 0), (r, c + 1), "inc", LAST, LAST)
    u4_down_right = add(u4, (r, c + 1), last & (lax.rem(c, 4) == 2), (r, c - 1), "inc", LAST, LAST)
    root_down, root_down_odd = [], []
    for sender, k, group in ((u2, 0, root_down), (col_odd, 1, root_down_odd)):
        for n, i in enumerate((0, 1, 2)):
            mine = hub & (x == i) & (parity == k)
            like = root_down[n] if k else None
            group.append(add(sender, (8 * i + 7, c), mine, (31, c), "inc_root", LAST, HUB, like))
    root_side = add(u2, (r, c + 1), col_odd, (r, c - 1), "inc_root", LAST, LAST)
    n32_k_left = add(n32, (r - 8, c), x0, (r + 8, c), "k_node", HUB, HUB)
    n32_k_right = add(n32, (r + 8, c), x2, (r - 8, c), "k_node", HUB, HUB)
    n16_k = add(n16, (r + 8, c), lead, (r - 8, c), "k_hub", HUB, HUB)
    n8_k_left = add(n8, (r - 2, c), y == 1, (r + 2, c), "k_node")
    n8_k_right = add(n8, (r + 2, c), y == 5, (r - 2, c), "k_node")
    n4_k_left = add(n4, (r - 1, c), (y == 0) | (y == 4), (r + 1, c), "k_node")
    n4_k_right = add(n4, (r + 1, c), (y == 2) | (y == 6), (r - 1, c), "k_node")
    n2_k = add(n2, (r + 1, c), odd, (r - 1, c), "k_leaf")
    hub_down = [
        add(hub, (r + (i - 7), c), y == i, (r + (7 - i), c), "inc_hub", HUB, ANY)
        for i in (0, 3, 1, 5, 2, 4, 6)
    ]
    net.greet()

    lower = pl.ds(0, RANK)
    upper = pl.ds(RANK, RANK)
    near = pl.ds(0, ROWS)
    far = pl.ds(ROWS, ROWS)
    left, right = (merged, 0), (merged, 1)

    @pl.when(block)
    def _():
        net.meet()

    copies[4].wait()
    top_send.start(ni.at[0], top)

    copies[2].wait()
    hot_leaf = one_hot(lord)
    copies[3].wait()
    el = mm(li[1], li[0]).astype(BF16)
    copies[1].wait()
    copies[0].wait()
    rotated = mm(lo[0], rhs[...])
    high = rotated.astype(BF16)
    rest = (rotated - high.astype(F32)).astype(BF16)
    both = tn(hot_leaf, jnp.concatenate([high, rest], axis=1))
    rotated = both[:, :RHS] + both[:, RHS:]
    elim_leaf[...] = rotated[:RANK].astype(BF16)
    skel_leaf[...] = (rotated[RANK:] - mm(el, elim_leaf[...])).T.astype(BF16)

    @pl.when(jnp.logical_not(block))
    def _():
        net.meet()

    for part in range(PARTS):
        leaf_up.start(skel_leaf, right, part)
    for copy in copies[7:]:
        copy.start()

    @pl.when(even)
    def _():
        merged[slab(0)] = skel_leaf[...]

    copies[5].wait()
    hot_node = one_hot(nord)
    copies[6].wait()
    gathered = tn(no[0], hot_node)
    p1_t[...] = gathered[:, :RANK].astype(BF16)
    el = mm(ni[1], ni[0]).astype(BF16)
    s_t[...] = (gathered[:, RANK:] - nt(p1_t[...], el)).astype(BF16)
    s_to_hub.start(s_t, s_hub)

    s_left.start(s_t.at[lower], s_half)
    s_right.start(s_t.at[upper], s_half)
    s_exchange.start(s_t, s_other)
    for i, m in enumerate(s_direct):
        m.start(s_t, s_late.at[i // 2])

    copies[7].wait()
    copies[8].wait()
    placed = mm(no[1], hot_node).astype(BF16)
    q1[...] = placed[:, :RANK]
    uf = mm(ni[3], ni[2]).astype(BF16)
    h_node[...] = (placed[:, RANK:].astype(F32) - mm(q1[...], uf)).astype(BF16)

    def upper_setup():
        @pl.when(u8 | u16)
        def _():
            ul = mm(ni[3], ni[0]).astype(BF16)
            big_g[...] = mm(q1[...], nt(ul, p1_t[...]).astype(BF16))

        net.arrived(u16, top, "top")

        @pl.when(u16)
        def _():
            m_top[...] = (
                big_g[...] + mm(h_node[...], nt(top[...], s_t[...]).astype(BF16))
            ).astype(BF16)

        m_top_left.start(m_top.at[lower], m_in)
        m_top_right.start(m_top.at[upper], m_in)

    def upper_map():
        net.arrived(u8, m_in, "m_top")
        net.arrived(u8, s_other, "s_other")

        def four_rows(own, other, mine):
            wide = jnp.concatenate(
                [nt(m_in[:, own], s_t[...]), nt(m_in[:, other], s_other[...])], axis=1
            ).astype(BF16)
            full = mm(h_node[...], wide)
            m_rows[:, pl.ds(mine * ROWS, ROWS)] = (full[:, :ROWS] + big_g[...]).astype(BF16)
            m_rows[:, pl.ds((1 - mine) * ROWS, ROWS)] = full[:, ROWS:].astype(BF16)

        @pl.when(last & (c == 3))
        def _():
            four_rows(lower, upper, 0)

        @pl.when(last & (c == 11))
        def _():
            four_rows(upper, lower, 1)

        for child, ms in ((lower, m_left), (upper, m_right)):
            ms["m_far"].start(m_rows.at[child, far], m_map.at[:, far])
            ms["m_near"].start(m_rows.at[child, near], m_map.at[:, near])

    upper_setup()

    net.arrived(n16, s_half, "s_half")

    @pl.when(n16)
    def _():
        both_m = mm(s_t[...], s_half[...]).astype(BF16)
        m_hub[...] = both_m[:RANK]
        m_out[...] = both_m[RANK:]

    m_to_hub.start(m_out, m_hub)

    net.arrived(lead, m_hub, "m_hub")
    net.arrived(hub, s_hub, "s_hub")

    @pl.when(hub)
    def _():
        cm_t[...] = mm(s_hub[...], m_hub[...]).astype(BF16)

    for part in range(PARTS):
        cut = rows_of(part)
        net.arrived(hub, (hb, 0), "hb_left", part)
        net.arrived(hub, (hb, 1), "hb_right", part)

        @pl.when(hub)
        def _():
            own = mm(hb[slab(0, part)], cm_t[lower]) + mm(hb[slab(1, part)], cm_t[upper])
            part_own[cut] = own
            skel_hub[cut] = own.astype(BF16)

        for i, m in enumerate(part_up):
            m.start(skel_hub, (parts, i), part)

    @pl.when(hub)
    def _():
        skel_eight[...] = (
            mm(hb[slab(0)], s_hub[lower]) + mm(hb[slab(1)], s_hub[upper])
        ).astype(BF16)

    for part in range(PARTS):
        n8_up.start(skel_eight, right, part)

    @pl.when(n16)
    def _():
        merged[slab(0)] = skel_eight[...]

    upper_map()

    for part in range(PARTS):
        cut = rows_of(part)

        for i in range(3):
            net.arrived(last, (parts, i), f"part{i}", part)

        @pl.when(last)
        def _():
            total = part_own[cut]
            for i in range(3):
                total = total + parts[slab(i, part)].astype(F32)
            skel_root[cut] = total.astype(BF16)

        col_up.start(skel_root, right, part)

        @pl.when(u2)
        def _():
            merged[slab(0, part)] = skel_root[cut]

        net.arrived(n4 | n8 | n32 | u4, left, "left", part)
        net.arrived(node, right, "right", part)

        @pl.when(node)
        def _():
            skel_node[cut] = (
                mm(merged[slab(0, part)], s_t[lower]) + mm(merged[slab(1, part)], s_t[upper])
            ).astype(BF16)

        n4_hub_left.start(skel_node, (hb, 0), part)
        n4_hub_right.start(skel_node, (hb, 1), part)
        n2_left.start(skel_node, left, part)
        n2_right.start(skel_node, right, part)
        for i, m in enumerate(direct[1]):
            m.start(skel_node, (late, i), part)
        for i, m in enumerate(direct[5]):
            m.start(skel_node, (late, i), part)
        u2_left.start(skel_node, left, part)
        u2_right.start(skel_node, right, part)
        for m in peer:
            m.start(skel_node, (peers, m.index), part)
        n16_left.start(skel_node, left, part)
        n16_right.start(skel_node, right, part)

    for part in range(PARTS):
        n4_left.start(skel_node, left, part)
        n4_right.start(skel_node, right, part)

    @pl.when(node)
    def _():
        eliminated = mm(merged[slab(0)], p1_t[lower]) + mm(merged[slab(1)], p1_t[upper])
        reduced = nt(eliminated.astype(BF16), ni[0]).astype(BF16)
        solved = nt(reduced, ni[3]).astype(BF16)
        g_node[...] = nt(solved, q1[...])

    for p in (1, 5, 9, 13):

        @pl.when(last & (c == p))
        def _(p=p):
            peers[slab(p // 4)] = skel_node[...]

    net.arrived(u4, m_map.at[:, far], "m_far")
    for i in range(2):
        net.arrived(early4, s_late.at[i], f"s_late{i}")

    @pl.when(early4)
    def _():
        for i in range(2):
            m_late[pl.ds(i * ROWS, ROWS)] = nt(
                s_late[i], m_map[:, pl.ds(ROWS + i * RANK, RANK)]
            ).astype(BF16)

    net.arrived(u4, m_map.at[:, near], "m_near")

    def peer_arrivals(nodes, part):
        for i, p in enumerate((1, 5, 9, 13)):
            takers = [d for d in nodes if d != p and (p < 8 or d > 8)]
            if takers:
                net.arrived(last & any_of(c, takers), (peers, i), f"peer{i}", part)

    for part in range(PARTS):
        peer_arrivals((1, 5), part)

    @pl.when(early4)
    def _():
        part_near[...] = nt(peers[slab(0)], m_map[:, pl.ds(0, RANK)]) + nt(peers[slab(1)], m_map[:, pl.ds(RANK, RANK)])

    takes = n2 | n4 | n16 | u2
    for part in range(PARTS):
        cut = rows_of(part)

        for i in range(4):
            net.arrived(early4, (late, i), f"late{i}", part)
        peer_arrivals((9, 13), part)

        @pl.when(early4)
        def _():
            total = part_near[cut]
            for i in range(4):
                total = total + mm(late[slab(i, part)], m_late[pl.ds(i * RANK, RANK)])
            inc_node[cut] = total.astype(BF16)

        @pl.when(late4)
        def _():
            total = nt(peers[slab(0, part)], m_map[:, pl.ds(0, RANK)])
            for i in range(1, 4):
                total = total + nt(peers[slab(i, part)], m_map[:, pl.ds(i * RANK, RANK)])
            inc_node[cut] = total.astype(BF16)

        net.arrived(takes, inc_node, "inc", part)

        @pl.when(takes | u4)
        def _():
            full = (g_node[cut] + nt(inc_node[cut], h_node[...])).astype(BF16)
            values[slab(0, part)] = full[:, :RANK]
            values[slab(1, part)] = full[:, RANK:]

        @pl.when(n8 | n32)
        def _():
            full = g_node[cut].astype(BF16)
            values[slab(0, part)] = full[:, :RANK]
            values[slab(1, part)] = full[:, RANK:]

        first, second = (values, 0), (values, 1)

        u4_down_right.start(second, inc_node, part)
        u4_down_left.start(first, inc_node, part)
        root_side.start(second, inc_root, part)
        for m in root_down:
            m.start(first, inc_root, part)
        n32_down_left.start(first, inc_node, part)
        n32_down_right.start(second, inc_node, part)
        n16_down.start(second, loc_hub, part)
        n8_down_left.start(first, inc_node, part)
        n8_down_right.start(second, inc_node, part)
        n4_down_left.start(first, inc_node, part)
        n4_down_right.start(second, inc_node, part)
        n2_down.start(second, inc_leaf, part)

        @pl.when(u2)
        def _():
            inc_root[cut] = values[slab(0, part)]

        @pl.when(n16)
        def _():
            loc_hub[cut] = values[slab(0, part)]

        @pl.when(n2)
        def _():
            inc_leaf[cut] = values[slab(0, part)]

    passes = n16 | n4 | n2

    n32_k_left.start(h_node.at[lower], k_node)
    n32_k_right.start(h_node.at[upper], k_node)
    n8_k_left.start(h_node.at[lower], k_node)
    n8_k_right.start(h_node.at[upper], k_node)
    net.arrived(passes, k_node, "k_node")

    @pl.when(passes)
    def _():
        kv[...] = mm(h_node[...], k_node[...]).astype(BF16)

    n16_k.start(kv.at[upper], k_hub)
    n4_k_left.start(kv.at[lower], k_node)
    n4_k_right.start(kv.at[upper], k_node)
    n2_k.start(kv.at[upper], k_leaf)

    @pl.when(n16)
    def _():
        k_hub[...] = kv[lower]

    @pl.when(n2)
    def _():
        k_leaf[...] = kv[lower]

    copies[9].wait()
    copies[10].wait()

    def leaf_down():
        placed = mm(lo[1], one_hot(lord)).astype(BF16)
        first = placed[:, :RANK]
        uf = mm(li[3], li[2]).astype(BF16)
        h = (placed[:, RANK:].astype(F32) - mm(first, uf)).astype(BF16)
        reduced = mm(li[0], elim_leaf[...]).astype(BF16)
        g = mm(first, mm(li[3], reduced).astype(BF16))
        for part in range(PARTS):
            net.arrived(odd, inc_leaf, "inc_leaf", part)
        g_leaf[...] = g + nt(h, inc_leaf[...])
        net.arrived(odd, k_leaf, "k_leaf")
        h_leaf[...] = mm(h, k_leaf[...]).astype(BF16)

    pl.when(jnp.logical_not(last))(leaf_down)

    for part in range(PARTS):
        cut = rows_of(part)
        net.arrived(col_odd | (hub & (x < 3)), inc_root, "inc_root", part)
        for m in root_down_odd:
            m.start(inc_root, inc_root, part)
        if part == 0:
            net.arrived(lead, k_hub, "k_hub")
            for each in range(PARTS):
                net.arrived(lead, loc_hub, "loc_hub", each)

        @pl.when(hub)
        def _():
            inc_hub[cut] = (loc_hub[cut].astype(F32) + nt(inc_root[cut], k_hub[...])).astype(BF16)

        for m in hub_down:
            m.start(inc_hub, inc_hub, part)
    pl.when(last)(leaf_down)

    net.finish([m for m in net.messages if m not in hub_down])
    for part in range(PARTS):
        net.arrived(low, inc_hub, "inc_hub", part)
    out[0, 0] = (g_leaf[...] + nt(h_leaf[...], inc_hub[...])).astype(BF16)
    net.finish(hub_down)


def solution(mesh):
    vm = pltpu.VMEM
    vector = vm((RHS, RANK), BF16)
    pair = vm((2 * RHS, RANK), BF16)
    square = vm((RANK, RANK), BF16)
    wide = vm((RANK, ROWS), BF16)
    tall = vm((ROWS, RANK), BF16)
    scratch = [
        vm((ROWS, RHS), BF16),
        vm((2, ROWS, ROWS), BF16),
        vm((4, RANK, RANK), BF16),
        vm((1, ROWS), jnp.int32),
        vm((2, ROWS, ROWS), BF16),
        vm((4, RANK, RANK), BF16),
        vm((1, ROWS), jnp.int32),
        vm((RANK, RHS), BF16),
        vector,
        pair,
        vector,
        square,
        vector,
        vector,
        pair,
        tall,
        tall,
        vm((RHS, ROWS), F32),
        tall,
        vm((ROWS, RHS), F32),
        tall,
        tall,
        pair,
        tall,
        square,
        square,
        square,
        square,
        vm((3 * RHS, RANK), BF16),
        vm((RHS, RANK), F32),
        vector,
        vector,
        tall,
        vector,
        vector,
        vector,
        square,
        square,
        tall,
        vm((ROWS, ROWS), F32),
        vm((ROWS, ROWS), BF16),
        wide,
        tall,
        vm((RANK, 4 * RANK), BF16),
        vm((ROWS, 4 * RANK), BF16),
        vm((4 * RHS, RANK), BF16),
        vm((2, ROWS, RANK), BF16),
        vm((4 * RHS, RANK), BF16),
        vm((4 * RANK, RANK), BF16),
        vm((RHS, RANK), F32),
        vector,
        pltpu.SemaphoreType.DMA((11,)),
        pltpu.SemaphoreType.DMA((LANES,)),
        pltpu.SemaphoreType.DMA((SLOTS,)),
    ]
    call = pl.pallas_call(
        kernel,
        out_shape=jax.ShapeDtypeStruct((1, 1, ROWS, RHS), BF16),
        in_specs=[pl.BlockSpec(memory_space=pltpu.HBM)] * 7,
        out_specs=pl.BlockSpec(memory_space=pltpu.VMEM),
        scratch_shapes=scratch,
        compiler_params=pltpu.CompilerParams(
            collective_id=0, has_side_effects=True, vmem_limit_bytes=40 * 1024 * 1024
        ),
        name="tree",
    )

    def local(*args):
        return call(*[pltpu.with_memory_space_constraint(a, pltpu.HBM) for a in args])

    in_specs = (
        P("col", "row", None, None),
        P("col", "row", None, None, None),
        P("col", "row", None, None, None),
        P("col", "row", None),
        P("col", "row", None, None, None),
        P("col", "row", None, None, None),
        P("col", "row", None),
    )
    out_specs = P("col", "row", None, None)
    return jax.shard_map(local, mesh=mesh, in_specs=in_specs, out_specs=out_specs, check_vma=False)
```

```python
import functools

import jax
import jax.numpy as jnp
from jax import lax
from jax.experimental import pallas as pl
from jax.experimental.pallas import tpu as pltpu
from jax.sharding import PartitionSpec as P

MESH = pl.DeviceIdType.MESH
BF16 = jnp.bfloat16
F32 = jnp.float32
RANK = 256
ROWS = 512
RHS = 128
PARTS = 2
CUT = RHS // PARTS


def mm(a, b):
    return jnp.dot(a, b, preferred_element_type=F32)


def nt(a, b):
    return lax.dot_general(a, b, (((1,), (1,)), ((), ())), preferred_element_type=F32)


def tn(a, b):
    return lax.dot_general(a, b, (((0,), (0,)), ((), ())), preferred_element_type=F32)


def one_hot(order_ref):
    rows = lax.broadcasted_iota(jnp.int32, (ROWS, ROWS), 0)
    return jnp.where(rows == order_ref[...], 1.0, 0.0).astype(BF16)


def any_of(value, choices):
    return functools.reduce(jnp.logical_or, [value == p for p in choices])


VECTORS = (
    "left", "right", "inc", "inc_leaf", "hb_left", "hb_right", "part0", "part1", "part2",
    "loc_hub", "inc_root", "inc_hub", "peer0", "peer1", "peer2", "peer3", "late0",
    "late1", "late2", "late3",
)
MATRICES = (
    "top", "s_hub", "m_hub", "s_half", "k_hub", "k_node", "k_leaf", "m_top", "s_other",
    "m_near", "m_far", "s_late0", "s_late1",
)
SLOT = {name: PARTS * i for i, name in enumerate(VECTORS)}
SLOT.update({name: PARTS * len(VECTORS) + i for i, name in enumerate(MATRICES)})
SLOTS = PARTS * len(VECTORS) + len(MATRICES)
LANES = 120
ANY, HUB, LAST = range(3)


def rows_of(part):
    return pl.ds(part * CUT, CUT)


def slab(index, part=None):
    start, size = index * RHS, RHS
    if part is not None:
        start, size = start + part * CUT, CUT
    if not isinstance(index, int):
        start = pl.multiple_of(start, CUT)
    return pl.ds(start, size)


def piece(ref, part):
    if isinstance(ref, tuple):
        return ref[0].at[slab(ref[1], part)]
    return ref.at[rows_of(part)]


class Message:
    def __init__(self, net, out, dst, into, src, slot, out_zone, in_zone, like):
        self.net, self.out, self.dst, self.into, self.src = net, out, dst, into, src
        self.slot, self.out_zone, self.in_zone = slot, out_zone, in_zone
        self.wide = slot in VECTORS
        if like is None:
            self.lane = net.lanes
            net.lanes += PARTS if self.wide else 1
        else:
            self.lane = like.lane
        self.copies = []
        net.messages.append(self)

    def start(self, src_ref, dst_ref, part=None):
        shift = 0
        if self.wide:
            src_ref, dst_ref, shift = piece(src_ref, part), piece(dst_ref, part), part
        copy = pltpu.make_async_remote_copy(
            src_ref=src_ref,
            dst_ref=dst_ref,
            send_sem=self.net.send_sem.at[self.lane + shift],
            recv_sem=self.net.recv_sem.at[SLOT[self.slot] + shift],
            device_id=self.dst,
            device_id_type=MESH,
        )
        self.copies.append(copy)
        pl.when(self.out)(copy.start)

    def finish(self):
        @pl.when(self.out)
        def _():
            for copy in self.copies:
                copy.wait_send()


class Net:
    def __init__(self, send_sem, recv_sem):
        self.messages, self.lanes = [], 0
        self.send_sem, self.recv_sem = send_sem, recv_sem
        c = lax.axis_index("col")
        self.partner = (lax.axis_index("row"), c + 1 - 2 * lax.rem(c, 2))

    def add(self, out, dst, into, src, slot, out_zone=ANY, in_zone=ANY, like=None):
        return Message(self, out, dst, into, src, slot, out_zone, in_zone, like)

    def by_zone(self, zone_of, act):
        def run(zone):
            for m in self.messages:
                if zone_of(m) == zone:
                    act(m)

        run(ANY)
        run(HUB)
        run(LAST)

    def greet(self):
        barrier = pltpu.get_barrier_semaphore()

        def act(m):
            @pl.when(m.into)
            def _():
                pl.semaphore_signal(barrier, inc=1, device_id=m.src, device_id_type=MESH)

        self.by_zone(lambda m: m.in_zone, act)
        self.count = sum(m.out.astype(jnp.int32) for m in self.messages)

    def meet(self):
        pl.semaphore_wait(pltpu.get_barrier_semaphore(), self.count)

    def arrived(self, cond, ref, slot, part=None):
        shift = 0
        if slot in VECTORS:
            ref, shift = piece(ref, part), part
        copy = pltpu.make_async_remote_copy(
            src_ref=ref,
            dst_ref=ref,
            send_sem=self.send_sem.at[0],
            recv_sem=self.recv_sem.at[SLOT[slot] + shift],
            device_id=self.partner,
            device_id_type=MESH,
        )
        pl.when(cond)(copy.wait_recv)

    def finish(self, messages):
        for m in messages:
            m.finish()


def kernel(
    rhs_h, lo_h, li_h, lord_h, no_h, ni_h, nord_h, out,
    rhs, lo, li, lord, no, ni, nord,
    elim_leaf, skel_leaf, merged, skel_node, top, inc_node, inc_leaf, values,
    s_t, h_node, g_node, h_leaf, g_leaf, p1_t, q1,
    hb, s_hub, m_hub, m_out, s_half, k_hub, parts, part_own, skel_hub, skel_eight, cm_t, loc_hub,
    inc_root, inc_hub, k_node, k_leaf, kv, big_g, m_top, m_in, s_other, m_map, m_rows, peers,
    s_late, late, m_late, part_near, skel_root, part_left,
    load_sem, send_sem, recv_sem,
):
    r = lax.axis_index("row")
    c = lax.axis_index("col")
    x = r // 8
    y = lax.rem(r, 8)
    parity = lax.rem(c, 2)
    even = lax.rem(y, 2) == 0
    odd = jnp.logical_not(even)
    n2 = even
    n4 = (y == 1) | (y == 5)
    n8 = y == 3
    hub = y == 7
    low = jnp.logical_not(hub)
    x0, x1, x2 = hub & (x == 0), hub & (x == 1), hub & (x == 2)
    n16 = x0 | x2
    n32 = x1
    last = hub & (x == 3)
    lead = x1 | last
    u2 = last & (parity == 0)
    col_odd = last & (parity == 1)
    u4 = last & (lax.rem(c, 4) == 1)
    u8 = last & (lax.rem(c, 8) == 3)
    u16 = last & (c == 7)
    block = last & (c == 15)
    early4 = last & ((c == 1) | (c == 5))
    late4 = last & ((c == 9) | (c == 13))
    node = low | n16 | n32 | u2 | u4

    loads = [
        (lo_h.at[0, 0, 0], lo.at[0]),
        (rhs_h.at[0, 0], rhs),
        (lord_h.at[0], lord),
        (li_h.at[0, 0, pl.ds(0, 2)], li.at[pl.ds(0, 2)]),
        (ni_h.at[0, 0, pl.ds(0, 2)], ni.at[pl.ds(0, 2)]),
        (nord_h.at[0], nord),
        (no_h.at[0, 0, 0], no.at[0]),
        (no_h.at[0, 0, 1], no.at[1]),
        (ni_h.at[0, 0, pl.ds(2, 2)], ni.at[pl.ds(2, 2)]),
        (lo_h.at[0, 0, 1], lo.at[1]),
        (li_h.at[0, 0, pl.ds(2, 2)], li.at[pl.ds(2, 2)]),
    ]
    copies = [
        pltpu.make_async_copy(src, dst, load_sem.at[i]) for i, (src, dst) in enumerate(loads)
    ]
    for copy in copies[:7]:
        copy.start()

    net = Net(send_sem, recv_sem)
    add = net.add
    leaf_up = add(odd, (r - 1, c), even, (r + 1, c), "right")
    n2_left = add((y == 0) | (y == 4), (r + 1, c), n4, (r - 1, c), "left")
    n2_right = add((y == 2) | (y == 6), (r - 1, c), n4, (r + 1, c), "right", like=n2_left)
    n4_hub_left = add(y == 1, (r + 6, c), hub, (r - 6, c), "hb_left", ANY, HUB)
    n4_hub_right = add(y == 5, (r + 2, c), hub, (r - 2, c), "hb_right", ANY, HUB, n4_hub_left)
    n4_left = add(y == 1, (r + 2, c), n8, (r - 2, c), "left")
    n4_right = add(y == 5, (r - 2, c), n8, (r + 2, c), "right", like=n4_left)
    s_to_hub = add(n8, (r + 4, c), hub, (r - 4, c), "s_hub", ANY, HUB)
    s_left = add(x1, (r - 8, c), x0, (r + 8, c), "s_half", HUB, HUB)
    s_right = add(x1, (r + 8, c), x2, (r - 8, c), "s_half", HUB, HUB)
    m_to_hub = add(n16, (r + 8, c), lead, (r - 8, c), "m_hub", HUB, HUB)
    part_up = [
        add(hub & (x == i), (31, c), last, (8 * i + 7, c), f"part{i}", HUB, LAST) for i in range(3)
    ]
    col_up = add(col_odd, (r, c - 1), u2, (r, c + 1), "right", LAST, LAST)
    n8_up = add(lead, (r - 8, c), n16, (r + 8, c), "right", HUB, HUB)
    n16_left = add(x0, (r + 8, c), n32, (r - 8, c), "left", HUB, HUB)
    n16_right = add(x2, (r - 8, c), n32, (r + 8, c), "right", HUB, HUB, n16_left)
    u2_left = add(last & (lax.rem(c, 4) == 0), (r, c + 1), u4, (r, c - 1), "left", LAST, LAST)
    u2_right = add(last & (lax.rem(c, 4) == 2), (r, c - 1), u4, (r, c + 1), "right", LAST, LAST)

    def chosen(sources, dst, into, src, slot, like=None):
        out, into = last & any_of(c, sources), last & any_of(c, into)
        return add(out, dst, into, src, slot, LAST, LAST, like)

    direct = {1: [], 5: []}
    for d, ms in direct.items():
        for i, p in enumerate((8, 10, 12, 14)):
            ms.append(chosen((p,), (r, d), (d,), (r, p), f"late{i}", ms[0] if ms else None))
    s_direct = [
        chosen((p,), (r, d), (d,), (r, p), f"s_late{i}") for i, p in enumerate((9, 13)) for d in (1, 5)
    ]
    peer = []
    for p, others in ((1, (9, 5, 13)), (5, (13, 1, 9)), (9, (13,)), (13, (9,))):
        for n, d in enumerate(others):
            like = peer[n] if p > 1 else None
            peer.append(chosen((p,), (r, d), (d,), (r, p), f"peer{p // 4}", like))
            peer[-1].index = p // 4
    top_send = chosen((15,), (r, c - 8), (7,), (r, c + 8), "top")
    m_top_left = chosen((7,), (r, c - 4), (3,), (r, c + 4), "m_top")
    m_top_right = chosen((7,), (r, c + 4), (11,), (r, c - 4), "m_top")
    s_exchange = chosen(
        (3, 11), (r, lax.rem(c + 8, 16)), (3, 11), (r, lax.rem(c + 8, 16)), "s_other"
    )
    m_left = {n: chosen((3, 11), (r, c - 2), (1, 9), (r, c + 2), n) for n in ("m_far", "m_near")}
    m_right = {n: chosen((3, 11), (r, c + 2), (5, 13), (r, c - 2), n) for n in ("m_far", "m_near")}
    n32_down_left = add(n32, (r - 8, c), x0, (r + 8, c), "inc", HUB, HUB)
    n32_down_right = add(n32, (r + 8, c), x2, (r - 8, c), "inc", HUB, HUB)
    n16_down = add(n16, (r + 8, c), lead, (r - 8, c), "loc_hub", HUB, HUB)
    n8_down_left = add(n8, (r - 2, c), y == 1, (r + 2, c), "inc")
    n8_down_right = add(n8, (r + 2, c), y == 5, (r - 2, c), "inc")
    n4_down_left = add(n4, (r - 1, c), (y == 0) | (y == 4), (r + 1, c), "inc")
    n4_down_right = add(n4, (r + 1, c), (y == 2) | (y == 6), (r - 1, c), "inc")
    n2_down = add(n2, (r + 1, c), odd, (r - 1, c), "inc_leaf")
    u4_down_left = add(u4, (r, c - 1), last & (lax.rem(c, 4) == 0), (r, c + 1), "inc", LAST, LAST)
    u4_down_right = add(u4, (r, c + 1), last & (lax.rem(c, 4) == 2), (r, c - 1), "inc", LAST, LAST)
    root_down, root_down_odd = [], []
    for sender, k, group in ((u2, 0, root_down), (col_odd, 1, root_down_odd)):
        for n, i in enumerate((0, 1, 2)):
            mine = hub & (x == i) & (parity == k)
            like = root_down[n] if k else None
            group.append(add(sender, (8 * i + 7, c), mine, (31, c), "inc_root", LAST, HUB, like))
    root_side = add(u2, (r, c + 1), col_odd, (r, c - 1), "inc_root", LAST, LAST)
    n32_k_left = add(n32, (r - 8, c), x0, (r + 8, c), "k_node", HUB, HUB)
    n32_k_right = add(n32, (r + 8, c), x2, (r - 8, c), "k_node", HUB, HUB)
    n16_k = add(n16, (r + 8, c), lead, (r - 8, c), "k_hub", HUB, HUB)
    n8_k_left = add(n8, (r - 2, c), y == 1, (r + 2, c), "k_node")
    n8_k_right = add(n8, (r + 2, c), y == 5, (r - 2, c), "k_node")
    n4_k_left = add(n4, (r - 1, c), (y == 0) | (y == 4), (r + 1, c), "k_node")
    n4_k_right = add(n4, (r + 1, c), (y == 2) | (y == 6), (r - 1, c), "k_node")
    n2_k = add(n2, (r + 1, c), odd, (r - 1, c), "k_leaf")
    hub_down = [
        add(hub, (r + (i - 7), c), y == i, (r + (7 - i), c), "inc_hub", HUB, ANY)
        for i in (0, 3, 1, 5, 2, 4, 6)
    ]
    net.greet()

    lower = pl.ds(0, RANK)
    upper = pl.ds(RANK, RANK)
    near = pl.ds(0, ROWS)
    far = pl.ds(ROWS, ROWS)
    left, right = (merged, 0), (merged, 1)

    @pl.when(block)
    def _():
        net.meet()

    copies[4].wait()
    top_send.start(ni.at[0], top)

    copies[2].wait()
    hot_leaf = one_hot(lord)
    copies[3].wait()
    el = mm(li[1], li[0]).astype(BF16)
    copies[1].wait()
    copies[0].wait()
    rotated = mm(lo[0], rhs[...])
    high = rotated.astype(BF16)
    rest = (rotated - high.astype(F32)).astype(BF16)
    both = tn(hot_leaf, jnp.concatenate([high, rest], axis=1))
    rotated = both[:, :RHS] + both[:, RHS:]
    elim_leaf[...] = rotated[:RANK].astype(BF16)
    skel_leaf[...] = (rotated[RANK:] - mm(el, elim_leaf[...])).T.astype(BF16)

    @pl.when(jnp.logical_not(block))
    def _():
        net.meet()

    for part in range(PARTS):
        leaf_up.start(skel_leaf, right, part)
    for copy in copies[7:]:
        copy.start()

    @pl.when(even)
    def _():
        merged[slab(0)] = skel_leaf[...]

    copies[5].wait()
    hot_node = one_hot(nord)
    copies[6].wait()
    gathered = tn(no[0], hot_node)
    p1_t[...] = gathered[:, :RANK].astype(BF16)
    el = mm(ni[1], ni[0]).astype(BF16)
    s_t[...] = (gathered[:, RANK:] - nt(p1_t[...], el)).astype(BF16)
    s_to_hub.start(s_t, s_hub)

    s_left.start(s_t.at[lower], s_half)
    s_right.start(s_t.at[upper], s_half)
    s_exchange.start(s_t, s_other)
    for i, m in enumerate(s_direct):
        m.start(s_t, s_late.at[i // 2])

    copies[7].wait()
    copies[8].wait()
    placed = mm(no[1], hot_node).astype(BF16)
    q1[...] = placed[:, :RANK]
    uf = mm(ni[3], ni[2]).astype(BF16)
    h_node[...] = (placed[:, RANK:].astype(F32) - mm(q1[...], uf)).astype(BF16)

    def upper_setup():
        @pl.when(u8 | u16)
        def _():
            ul = mm(ni[3], ni[0]).astype(BF16)
            big_g[...] = mm(q1[...], nt(ul, p1_t[...]).astype(BF16))

        net.arrived(u16, top, "top")

        @pl.when(u16)
        def _():
            m_top[...] = (
                big_g[...] + mm(h_node[...], nt(top[...], s_t[...]).astype(BF16))
            ).astype(BF16)

        m_top_left.start(m_top.at[lower], m_in)
        m_top_right.start(m_top.at[upper], m_in)

    def upper_map():
        net.arrived(u8, m_in, "m_top")
        net.arrived(u8, s_other, "s_other")

        def four_rows(own, other, mine):
            wide = jnp.concatenate(
                [nt(m_in[:, own], s_t[...]), nt(m_in[:, other], s_other[...])], axis=1
            ).astype(BF16)
            full = mm(h_node[...], wide)
            m_rows[:, pl.ds(mine * ROWS, ROWS)] = (full[:, :ROWS] + big_g[...]).astype(BF16)
            m_rows[:, pl.ds((1 - mine) * ROWS, ROWS)] = full[:, ROWS:].astype(BF16)

        @pl.when(last & (c == 3))
        def _():
            four_rows(lower, upper, 0)

        @pl.when(last & (c == 11))
        def _():
            four_rows(upper, lower, 1)

        for child, ms in ((lower, m_left), (upper, m_right)):
            ms["m_far"].start(m_rows.at[child, far], m_map.at[:, far])
            ms["m_near"].start(m_rows.at[child, near], m_map.at[:, near])

    upper_setup()

    net.arrived(n16, s_half, "s_half")

    @pl.when(n16)
    def _():
        both_m = mm(s_t[...], s_half[...]).astype(BF16)
        m_hub[...] = both_m[:RANK]
        m_out[...] = both_m[RANK:]

    m_to_hub.start(m_out, m_hub)

    net.arrived(lead, m_hub, "m_hub")
    net.arrived(hub, s_hub, "s_hub")

    @pl.when(hub)
    def _():
        cm_t[...] = mm(s_hub[...], m_hub[...]).astype(BF16)

    for part in range(PARTS):
        cut = rows_of(part)
        net.arrived(hub, (hb, 0), "hb_left", part)

        @pl.when(hub)
        def _():
            part_left[cut] = mm(hb[slab(0, part)], cm_t[lower])

        net.arrived(hub, (hb, 1), "hb_right", part)

        @pl.when(hub)
        def _():
            own = part_left[cut] + mm(hb[slab(1, part)], cm_t[upper])
            part_own[cut] = own
            skel_hub[cut] = own.astype(BF16)

        for i, m in enumerate(part_up):
            m.start(skel_hub, (parts, i), part)

    @pl.when(hub)
    def _():
        skel_eight[...] = (
            mm(hb[slab(0)], s_hub[lower]) + mm(hb[slab(1)], s_hub[upper])
        ).astype(BF16)

    for part in range(PARTS):
        n8_up.start(skel_eight, right, part)

    @pl.when(n16)
    def _():
        merged[slab(0)] = skel_eight[...]

    upper_map()

    for part in range(PARTS):
        cut = rows_of(part)

        for i in range(3):
            net.arrived(last, (parts, i), f"part{i}", part)

        @pl.when(last)
        def _():
            total = part_own[cut]
            for i in range(3):
                total = total + parts[slab(i, part)].astype(F32)
            skel_root[cut] = total.astype(BF16)

        col_up.start(skel_root, right, part)

        @pl.when(u2)
        def _():
            merged[slab(0, part)] = skel_root[cut]

        net.arrived(n4 | n8 | n32 | u4, left, "left", part)

        @pl.when(node)
        def _():
            part_left[cut] = mm(merged[slab(0, part)], s_t[lower])

        net.arrived(node, right, "right", part)

        @pl.when(node)
        def _():
            skel_node[cut] = (part_left[cut] + mm(merged[slab(1, part)], s_t[upper])).astype(BF16)

        n4_hub_left.start(skel_node, (hb, 0), part)
        n4_hub_right.start(skel_node, (hb, 1), part)
        n2_left.start(skel_node, left, part)
        n2_right.start(skel_node, right, part)
        for i, m in enumerate(direct[1]):
            m.start(skel_node, (late, i), part)
        for i, m in enumerate(direct[5]):
            m.start(skel_node, (late, i), part)
        u2_left.start(skel_node, left, part)
        u2_right.start(skel_node, right, part)
        for m in peer:
            m.start(skel_node, (peers, m.index), part)
        n16_left.start(skel_node, left, part)
        n16_right.start(skel_node, right, part)

    for part in range(PARTS):
        n4_left.start(skel_node, left, part)
        n4_right.start(skel_node, right, part)

    @pl.when(node)
    def _():
        eliminated = mm(merged[slab(0)], p1_t[lower]) + mm(merged[slab(1)], p1_t[upper])
        reduced = nt(eliminated.astype(BF16), ni[0]).astype(BF16)
        solved = nt(reduced, ni[3]).astype(BF16)
        g_node[...] = nt(solved, q1[...])

    for p in (1, 5, 9, 13):

        @pl.when(last & (c == p))
        def _(p=p):
            peers[slab(p // 4)] = skel_node[...]

    net.arrived(u4, m_map.at[:, far], "m_far")
    for i in range(2):
        net.arrived(early4, s_late.at[i], f"s_late{i}")

    @pl.when(early4)
    def _():
        for i in range(2):
            m_late[pl.ds(i * ROWS, ROWS)] = nt(
                s_late[i], m_map[:, pl.ds(ROWS + i * RANK, RANK)]
            ).astype(BF16)

    net.arrived(u4, m_map.at[:, near], "m_near")

    def peer_arrivals(nodes, part):
        for i, p in enumerate((1, 5, 9, 13)):
            takers = [d for d in nodes if d != p and (p < 8 or d > 8)]
            if takers:
                net.arrived(last & any_of(c, takers), (peers, i), f"peer{i}", part)

    for part in range(PARTS):
        peer_arrivals((1, 5), part)

    @pl.when(early4)
    def _():
        part_near[...] = nt(peers[slab(0)], m_map[:, pl.ds(0, RANK)]) + nt(peers[slab(1)], m_map[:, pl.ds(RANK, RANK)])

    takes = n2 | n4 | n16 | u2
    for part in range(PARTS):
        cut = rows_of(part)

        for i in range(4):
            net.arrived(early4, (late, i), f"late{i}", part)
        peer_arrivals((9, 13), part)

        @pl.when(early4)
        def _():
            total = part_near[cut]
            for i in range(4):
                total = total + mm(late[slab(i, part)], m_late[pl.ds(i * RANK, RANK)])
            inc_node[cut] = total.astype(BF16)

        @pl.when(late4)
        def _():
            total = nt(peers[slab(0, part)], m_map[:, pl.ds(0, RANK)])
            for i in range(1, 4):
                total = total + nt(peers[slab(i, part)], m_map[:, pl.ds(i * RANK, RANK)])
            inc_node[cut] = total.astype(BF16)

        net.arrived(takes, inc_node, "inc", part)

        @pl.when(takes | u4)
        def _():
            full = (g_node[cut] + nt(inc_node[cut], h_node[...])).astype(BF16)
            values[slab(0, part)] = full[:, :RANK]
            values[slab(1, part)] = full[:, RANK:]

        @pl.when(n8 | n32)
        def _():
            full = g_node[cut].astype(BF16)
            values[slab(0, part)] = full[:, :RANK]
            values[slab(1, part)] = full[:, RANK:]

        first, second = (values, 0), (values, 1)

        u4_down_right.start(second, inc_node, part)
        u4_down_left.start(first, inc_node, part)
        root_side.start(second, inc_root, part)
        for m in root_down:
            m.start(first, inc_root, part)
        n32_down_left.start(first, inc_node, part)
        n32_down_right.start(second, inc_node, part)
        n16_down.start(second, loc_hub, part)
        n8_down_left.start(first, inc_node, part)
        n8_down_right.start(second, inc_node, part)
        n4_down_left.start(first, inc_node, part)
        n4_down_right.start(second, inc_node, part)
        n2_down.start(second, inc_leaf, part)

        @pl.when(u2)
        def _():
            inc_root[cut] = values[slab(0, part)]

        @pl.when(n16)
        def _():
            loc_hub[cut] = values[slab(0, part)]

        @pl.when(n2)
        def _():
            inc_leaf[cut] = values[slab(0, part)]

    passes = n16 | n4 | n2

    n32_k_left.start(h_node.at[lower], k_node)
    n32_k_right.start(h_node.at[upper], k_node)
    n8_k_left.start(h_node.at[lower], k_node)
    n8_k_right.start(h_node.at[upper], k_node)
    net.arrived(passes, k_node, "k_node")

    @pl.when(passes)
    def _():
        kv[...] = mm(h_node[...], k_node[...]).astype(BF16)

    n16_k.start(kv.at[upper], k_hub)
    n4_k_left.start(kv.at[lower], k_node)
    n4_k_right.start(kv.at[upper], k_node)
    n2_k.start(kv.at[upper], k_leaf)

    @pl.when(n16)
    def _():
        k_hub[...] = kv[lower]

    @pl.when(n2)
    def _():
        k_leaf[...] = kv[lower]

    copies[9].wait()
    copies[10].wait()

    def leaf_down():
        placed = mm(lo[1], one_hot(lord)).astype(BF16)
        first = placed[:, :RANK]
        uf = mm(li[3], li[2]).astype(BF16)
        h = (placed[:, RANK:].astype(F32) - mm(first, uf)).astype(BF16)
        reduced = mm(li[0], elim_leaf[...]).astype(BF16)
        g = mm(first, mm(li[3], reduced).astype(BF16))
        for part in range(PARTS):
            net.arrived(odd, inc_leaf, "inc_leaf", part)
        g_leaf[...] = g + nt(h, inc_leaf[...])
        net.arrived(odd, k_leaf, "k_leaf")
        h_leaf[...] = mm(h, k_leaf[...]).astype(BF16)

    pl.when(jnp.logical_not(last))(leaf_down)

    for part in range(PARTS):
        cut = rows_of(part)
        net.arrived(col_odd | (hub & (x < 3)), inc_root, "inc_root", part)
        for m in root_down_odd:
            m.start(inc_root, inc_root, part)
        if part == 0:
            net.arrived(lead, k_hub, "k_hub")
            for each in range(PARTS):
                net.arrived(lead, loc_hub, "loc_hub", each)

        @pl.when(hub)
        def _():
            inc_hub[cut] = (loc_hub[cut].astype(F32) + nt(inc_root[cut], k_hub[...])).astype(BF16)

        for m in hub_down:
            m.start(inc_hub, inc_hub, part)
    pl.when(last)(leaf_down)

    net.finish([m for m in net.messages if m not in hub_down])
    for part in range(PARTS):
        net.arrived(low, inc_hub, "inc_hub", part)
    out[0, 0] = (g_leaf[...] + nt(h_leaf[...], inc_hub[...])).astype(BF16)
    net.finish(hub_down)


def solution(mesh):
    vm = pltpu.VMEM
    vector = vm((RHS, RANK), BF16)
    pair = vm((2 * RHS, RANK), BF16)
    square = vm((RANK, RANK), BF16)
    wide = vm((RANK, ROWS), BF16)
    tall = vm((ROWS, RANK), BF16)
    scratch = [
        vm((ROWS, RHS), BF16),
        vm((2, ROWS, ROWS), BF16),
        vm((4, RANK, RANK), BF16),
        vm((1, ROWS), jnp.int32),
        vm((2, ROWS, ROWS), BF16),
        vm((4, RANK, RANK), BF16),
        vm((1, ROWS), jnp.int32),
        vm((RANK, RHS), BF16),
        vector,
        pair,
        vector,
        square,
        vector,
        vector,
        pair,
        tall,
        tall,
        vm((RHS, ROWS), F32),
        tall,
        vm((ROWS, RHS), F32),
        tall,
        tall,
        pair,
        tall,
        square,
        square,
        square,
        square,
        vm((3 * RHS, RANK), BF16),
        vm((RHS, RANK), F32),
        vector,
        vector,
        tall,
        vector,
        vector,
        vector,
        square,
        square,
        tall,
        vm((ROWS, ROWS), F32),
        vm((ROWS, ROWS), BF16),
        wide,
        tall,
        vm((RANK, 4 * RANK), BF16),
        vm((ROWS, 4 * RANK), BF16),
        vm((4 * RHS, RANK), BF16),
        vm((2, ROWS, RANK), BF16),
        vm((4 * RHS, RANK), BF16),
        vm((4 * RANK, RANK), BF16),
        vm((RHS, RANK), F32),
        vector,
        vm((RHS, RANK), F32),
        pltpu.SemaphoreType.DMA((11,)),
        pltpu.SemaphoreType.DMA((LANES,)),
        pltpu.SemaphoreType.DMA((SLOTS,)),
    ]
    call = pl.pallas_call(
        kernel,
        out_shape=jax.ShapeDtypeStruct((1, 1, ROWS, RHS), BF16),
        in_specs=[pl.BlockSpec(memory_space=pltpu.HBM)] * 7,
        out_specs=pl.BlockSpec(memory_space=pltpu.VMEM),
        scratch_shapes=scratch,
        compiler_params=pltpu.CompilerParams(
            collective_id=0, has_side_effects=True, vmem_limit_bytes=40 * 1024 * 1024
        ),
        name="tree",
    )

    def local(*args):
        return call(*[pltpu.with_memory_space_constraint(a, pltpu.HBM) for a in args])

    in_specs = (
        P("col", "row", None, None),
        P("col", "row", None, None, None),
        P("col", "row", None, None, None),
        P("col", "row", None),
        P("col", "row", None, None, None),
        P("col", "row", None, None, None),
        P("col", "row", None),
    )
    out_specs = P("col", "row", None, None)
    return jax.shard_map(local, mesh=mesh, in_specs=in_specs, out_specs=out_specs, check_vma=False)
```
